32 devices in a mesh: ctx: 8 (over z, x), head: 4 (over y, core).
Axes of the slice: x: 2, y: 2, z: 4, core: 2. Of those that a mesh axis runs over, the one named last changes fastest.
Arguments:
- queries: bfloat16 [2048, 8, 128], P('ctx', 'head'), may hold values from -6 to 6
- spikes: int32 [2048, 8, 128], P('ctx', 'head'), may hold values from 0 to 3
- values: bfloat16 [2048, 8, 128], P('ctx', 'head'), may hold values from -6 to 6
- threshold: float32 [128], replicated, may hold values from 0.05 to 0.5
- norm_gain: float32 [128], replicated, may hold values from 0.1 to 1.9
- document_ids: int32 [2048], P('ctx'), may hold values from 0 to 31, never falling along the last dimension, each value on 1 to 512 neighbouring positions
- cotangent: bfloat16 [2048, 8, 128], P('ctx', 'head'), may hold values from -6 to 6
Outputs:
- attended: bfloat16 [2048, 8, 128], P('ctx', 'head')
- query_grad: bfloat16 [2048, 8, 128], P('ctx', 'head')
- value_grad: bfloat16 [2048, 8, 128], P('ctx', 'head')
- threshold_grad: float32 [128], replicated
- gain_grad: float32 [128], replicated
The draws below stay inside these ranges and needn't reach their ends.
Inputs may be any that keep to these rules, and one draw needn't show every extreme that they name: `document_ids`: ids never fall along the context; each document holds 1 to 512 consecutive tokens, and one holds exactly 512.
All inputs are finite; a program needn't handle non-finite values.
Results may differ from the reference program's by a relative error of at most 0.011.
Values sent between devices are 32-bit elements; how exact they have to be, the bound alone decides.
No kernel may reach another device: no remote copies, remote signals or barrier semaphores. Data moves between devices by JAX's collectives and lax.ppermute only.
A program may use at most 128 MiB of HBM per device.

```python
import math
import jax
import jax.numpy as jnp
import numpy as np
from jax import lax

DK = 128
TOK_DEV = 256
TOKENS = 2048
HEADS = 8
DOCS = 32
N_CTX = 8


def place_ends(values, rng, low, largest):
    spot = [jax.random.randint(jax.random.fold_in(rng, axis), (), 0, length) for axis, length in enumerate(values.shape)]
    longest = values.shape.index(max(values.shape))
    next_to = spot[:longest] + [(spot[longest] + 1) % values.shape[longest]] + spot[longest + 1:]
    return values.at[tuple(spot)].set(low).at[tuple(next_to)].set(largest)


def levels(stream_key, dims, shards, smallest, top_value):
    level = 1.0
    for dim, shards_of in shards:
        heights = jax.random.uniform(jax.random.fold_in(jax.random.fold_in(stream_key, 6), dim), (shards_of,), jnp.float32, smallest / len(shards), top_value / len(shards))
        level = level * jnp.repeat(jnp.exp(heights), dims[dim] // shards_of).reshape((-1,) + (1,) * (len(dims) - 1 - dim))
    return level


def split_up(number_of, total, most, lean):
    portions = [(1 << 20) // math.isqrt(rank ** lean) + 1 for rank in range(2, number_of + 1)]
    surplus, counts = total - most - (number_of - 1), [1] * (number_of - 1)
    while surplus > 0:
        candidates = [i for i in range(number_of - 1) if counts[i] < most]
        whole, remaining = sum([portions[i] for i in candidates]), surplus
        for i in candidates:
            more = min(most - counts[i], max(1, remaining * portions[i] // whole), surplus)
            counts[i] = counts[i] + more
            surplus = surplus - more
    return np.array([most] + counts)


def uneven_parts(stream_key, number_of, total, reach, skew):
    if number_of == 2:
        one = jax.random.randint(stream_key, (), max(1, total - reach), min(reach, total - 1) + 1)
        return jnp.stack([one, total - one])
    lengths = jnp.asarray(split_up(number_of, total, reach, skew), jnp.int32)
    pairs = (number_of - 1) // 2
    giver, receiver = lengths[1:1 + 2 * pairs:2], lengths[2:2 + 2 * pairs:2]
    room = jnp.minimum(giver - 1, reach - receiver)
    moved = jax.random.randint(jax.random.fold_in(stream_key, 1), (pairs,), 0, 1 << 20) % (room + 1)
    lengths = lengths.at[1:1 + 2 * pairs:2].set(giver - moved).at[2:2 + 2 * pairs:2].set(receiver + moved)
    return lengths[jax.random.permutation(jax.random.fold_in(stream_key, 2), number_of)]


def bell_draw(rng, dims, deviation, reach, pieces=(), held_as=jnp.bfloat16):
    values = jax.random.normal(rng, dims, jnp.float32) * deviation
    if len(pieces) > 0:
        values = levels(rng, dims, pieces, -0.22, 0.18) * values
    return jnp.clip(values, min=-reach, max=reach).astype(held_as)


def setup_inputs(seed: int = 0) -> dict:
    keys = jax.random.split(jax.random.key(seed), 8)
    return {
        "queries": bell_draw(keys[0], (TOKENS, HEADS, DK), 1.0, 6.0, ((0, 8), (1, 4))),
        "spikes": place_ends(jax.random.randint(keys[1], (TOKENS, HEADS, DK), 0, 4), jax.random.fold_in(keys[1], 1), 0, 3).astype(jnp.int32),
        "values": bell_draw(keys[2], (TOKENS, HEADS, DK), 1.0, 6.0, ((0, 8), (1, 4))),
        "threshold": jnp.clip(jnp.exp(jax.random.uniform(keys[3], (DK,), jnp.float32, math.log(0.05), math.log(0.5))), 0.05, 0.5),
        "norm_gain": jnp.clip(1.0 + 0.18 * jax.random.normal(keys[4], (DK,), jnp.float32), 0.1, 1.9),
        "document_ids": jnp.searchsorted(jnp.cumsum(uneven_parts(keys[5], DOCS, TOKENS, TOKENS // 4, 2)), jnp.arange(TOKENS), side="right").astype(jnp.int32),
        "cotangent": bell_draw(keys[6], (TOKENS, HEADS, DK), 1.0, 6.0, ((0, 8), (1, 4))),
    }


def rounded(tensor):
    return lax.optimization_barrier(tensor.astype(jnp.bfloat16)).astype(jnp.float32)

def reference(queries, spikes, values, threshold, norm_gain, document_ids, cotangent):
    keys_bf = (spikes.astype(jnp.float32) * threshold).astype(jnp.bfloat16)
    block_shape = (N_CTX, TOK_DEV, HEADS, DK)
    query_blocks = queries.reshape(block_shape)
    key_blocks = keys_bf.reshape(block_shape)
    value_blocks = values.reshape(block_shape)
    spike_blocks = spikes.reshape(block_shape)
    cot_blocks = cotangent.reshape(block_shape)
    doc_blocks = document_ids.reshape(N_CTX, TOK_DEV)

    def forward_step(carry, items):
        state, marker = carry
        key_c, value_c, doc_c = items
        last_f = (doc_c == doc_c[-1]).astype(jnp.float32)[:, None, None]
        tail = jnp.einsum('thd,the->hde', key_c.astype(jnp.float32) * last_f, value_c.astype(jnp.float32))
        incoming = jnp.where(marker == doc_c[0], state, jnp.float32(0.0)).astype(jnp.bfloat16)
        new_state = tail + jnp.where(marker == doc_c[-1], state, jnp.float32(0.0))
        return ((new_state, doc_c[-1]), incoming)
    start = (jnp.zeros((HEADS, DK, DK), jnp.float32), jnp.int32(-1))
    ignored, carried_all = lax.scan(forward_step, start, (key_blocks, value_blocks, doc_blocks))
    position = jnp.arange(TOK_DEV, dtype=jnp.int32)

    def reverse_step(carry, items):
        state, marker = carry
        query_c, key_c, value_c, spike_c, cot_c, doc_c, carried = items
        qf = query_c.astype(jnp.float32)
        kf = key_c.astype(jnp.float32)
        vf = value_c.astype(jnp.float32)
        allowed = (position[None, :] <= position[:, None]) & (doc_c[:, None] == doc_c[None, :])
        in_first = (doc_c == doc_c[0]).astype(jnp.float32)[:, None, None]
        in_last = (doc_c == doc_c[-1]).astype(jnp.float32)[:, None, None]
        scores = rounded(jnp.where(allowed[None], jnp.einsum('shd,thd->hst', qf, kf), jnp.float32(0.0)))
        carried_f = carried.astype(jnp.float32)
        mixed_raw = qf + jnp.einsum('hst,thd->shd', scores, vf) + in_first * jnp.einsum('shd,hde->she', qf, carried_f)
        ratio = lax.rsqrt(lax.optimization_barrier(jnp.mean(mixed_raw * mixed_raw, axis=-1, keepdims=True)) + 1e-06)
        normed = mixed_raw * ratio
        attended = (normed * norm_gain).astype(jnp.bfloat16)
        cot_f = cot_c.astype(jnp.float32)
        upstream = cot_f * norm_gain
        gnorm = rounded(ratio * upstream - normed * ratio * lax.optimization_barrier(jnp.mean(normed * upstream, axis=-1, keepdims=True)))
        dscores = rounded(jnp.where(allowed[None], jnp.einsum('shd,thd->hst', gnorm, vf), jnp.float32(0.0)))
        tail_ret = jnp.einsum('shd,she->hde', qf * in_first, gnorm)
        returned = rounded(jnp.where(marker == doc_c[-1], state, jnp.float32(0.0)))
        query_grad = gnorm + jnp.einsum('hst,thd->shd', dscores, kf) + in_first * jnp.einsum('she,hde->shd', gnorm, carried_f)
        key_grad = jnp.einsum('hst,shd->thd', dscores, qf) + in_last * jnp.einsum('the,hde->thd', vf, returned)
        value_grad = jnp.einsum('hst,she->the', scores, gnorm) + in_last * jnp.einsum('thd,hde->the', kf, returned)
        thresh_term = lax.optimization_barrier(jnp.sum(spike_c.astype(jnp.float32) * key_grad, axis=(0, 1)))
        gain_term = lax.optimization_barrier(jnp.sum(cot_f * normed, axis=(0, 1)))
        new_state = tail_ret + jnp.where(marker == doc_c[0], state, jnp.float32(0.0))
        outputs = (attended, query_grad.astype(jnp.bfloat16), value_grad.astype(jnp.bfloat16), thresh_term, gain_term)
        return ((new_state, doc_c[0]), outputs)
    items = (query_blocks, key_blocks, value_blocks, spike_blocks, cot_blocks, doc_blocks, carried_all)
    ignored, results = lax.scan(reverse_step, start, items, reverse=True)
    full_shape = (TOKENS, HEADS, DK)
    scale = jnp.float32(1.0) / jnp.sqrt(jnp.float32(TOKENS * HEADS))
    attended = results[0].reshape(full_shape)
    query_grad = results[1].reshape(full_shape)
    value_grad = results[2].reshape(full_shape)
    threshold_grad = lax.optimization_barrier(jnp.sum(results[3], axis=0)) * scale
    gain_grad = lax.optimization_barrier(jnp.sum(results[4], axis=0)) * scale
    return (attended, query_grad, value_grad, threshold_grad, gain_grad)
```

```python
import functools
import math

import jax
import jax.numpy as jnp
from jax import lax
from jax.experimental import pallas as pl
from jax.experimental.pallas import tpu as pltpu
from jax.sharding import PartitionSpec as P

BF16 = jnp.bfloat16
F32 = jnp.float32
MARK_ROWS = 8
VMEM_LIMIT = 48 * 1024 * 1024


def row_iota(shape):
    return lax.broadcasted_iota(jnp.int32, shape, 0)


def col_iota(shape):
    return lax.broadcasted_iota(jnp.int32, shape, 1)


def dot_nn(a, b):
    return lax.dot_general(a, b, (((1,), (0,)), ((), ())), preferred_element_type=F32)


def dot_nt(a, b):
    return lax.dot_general(a, b, (((1,), (1,)), ((), ())), preferred_element_type=F32)


def dot_tn(a, b):
    return lax.dot_general(a, b, (((0,), (0,)), ((), ())), preferred_element_type=F32)


def head_docs(ids):
    return ids[:, :1]


def tail_docs(ids):
    return ids[:, ids.shape[1] - 1 :]


def first_rows(ids, heads, rows):
    count = jnp.sum((ids == head_docs(ids)).astype(jnp.int32), axis=1, keepdims=True)
    return row_iota((rows, 1)) < heads * count


def last_rows(ids, heads, rows):
    count = jnp.sum((ids != tail_docs(ids)).astype(jnp.int32), axis=1, keepdims=True)
    return row_iota((rows, 1)) >= heads * count


def split_heads(x, keep, heads):
    head = lax.rem(row_iota((x.shape[0], 1)), heads)
    return jnp.concatenate(
        [jnp.where(keep & (head == h), x, jnp.zeros_like(x)) for h in range(heads)], axis=1
    )


def pick_heads(parts, keep):
    heads = len(parts)
    head = lax.rem(row_iota((parts[0].shape[0], 1)), heads)
    out = jnp.zeros_like(parts[0])
    for h in range(heads):
        out = jnp.where(keep & (head == h), parts[h], out)
    return out


def put_message(out_ref, state, mark):
    count = state.shape[0]
    out_ref[:count, :] = state
    out_ref[count:, :] = jnp.broadcast_to(mark.astype(F32), (MARK_ROWS, out_ref.shape[1]))


def take_messages(refs, mark):
    total = None
    for ref in refs:
        count = ref.shape[0] - MARK_ROWS
        same = (ref[count : count + 1, :] == mark.astype(F32)).astype(F32)
        part = ref[:count, :] * same
        total = part if total is None else total + part
    return total.astype(BF16)


def tail_kernel(heads, spikes_ref, values_ref, threshold_ref, ids_ref, tail_ref):
    ids = ids_ref[...]
    rows = values_ref.shape[0]
    keys = (spikes_ref[...].astype(F32) * threshold_ref[...]).astype(BF16)
    spread = split_heads(keys, last_rows(ids, heads, rows), heads)
    put_message(tail_ref, dot_tn(spread, values_ref[...]), tail_docs(ids))


def inside_kernel(
    heads, queries_ref, spikes_ref, values_ref, threshold_ref, ids_ref,
    base_ref, scores_ref, mask_ref, keys_ref,
):
    rows = queries_ref.shape[0]
    tokens = ids_ref.shape[1]
    queries = queries_ref[...]
    keys = (spikes_ref[...].astype(F32) * threshold_ref[...]).astype(BF16)
    keys_ref[...] = keys
    ids = ids_ref[...].astype(F32)
    apart = row_iota((rows, tokens)) - heads * col_iota((rows, tokens))
    down = jnp.sum(
        jnp.where((apart >= 0) & (apart < heads), ids, 0.0), axis=1, keepdims=True
    )
    r = row_iota((rows, rows))
    c = col_iota((rows, rows))
    across = jnp.sum(jnp.where(r == c, down, 0.0), axis=0, keepdims=True)
    allowed = (c <= r) & (down == across) & (lax.rem(r - c, heads) == 0)
    scores = jnp.where(allowed, dot_nt(queries, keys), 0.0).astype(BF16)
    scores_ref[...] = scores
    mask_ref[...] = allowed.astype(BF16)
    base_ref[...] = queries.astype(F32) + dot_nn(scores, values_ref[...])


def middle_kernel(
    heads, hops, queries_ref, values_ref, cotangent_ref, base_ref, mask_ref, keys_ref,
    threshold_ref, gain_ref, ids_ref, *refs,
):
    received = refs[:hops]
    attended_ref, query_grad_ref, gnorm_ref, back_ref, partial_ref = refs[hops:]
    rows, width = queries_ref.shape
    ids = ids_ref[...]
    queries = queries_ref[...]
    first = first_rows(ids, heads, rows)
    carried = take_messages(received, head_docs(ids))
    states = [carried[h * width : (h + 1) * width, :] for h in range(heads)]
    mixed = base_ref[...] + pick_heads([dot_nn(queries, s) for s in states], first)
    ratio = lax.rsqrt(jnp.mean(mixed * mixed, axis=1, keepdims=True) + 1e-06)
    normed = mixed * ratio
    gain = gain_ref[...]
    attended_ref[...] = (normed * gain).astype(BF16)
    cotangent = cotangent_ref[...].astype(F32)
    upstream = cotangent * gain
    inner = jnp.mean(normed * upstream, axis=1, keepdims=True)
    gnorm = (ratio * upstream - normed * ratio * inner).astype(BF16)
    gnorm_ref[...] = gnorm
    put_message(back_ref, dot_tn(split_heads(queries, first, heads), gnorm), head_docs(ids))
    dscores = (dot_nt(gnorm, values_ref[...]) * mask_ref[...].astype(F32)).astype(BF16)
    mixing = dot_nn(dscores, keys_ref[...])
    mixing = mixing + pick_heads([dot_nt(gnorm, s) for s in states], first)
    query_grad_ref[...] = (gnorm.astype(F32) + mixing).astype(BF16)
    threshold_part = (
        jnp.sum(queries.astype(F32) * mixing, axis=0, keepdims=True) / threshold_ref[...]
    )
    gain_part = jnp.sum(cotangent * normed, axis=0, keepdims=True)
    both = jnp.concatenate([threshold_part, gain_part], axis=0)
    partial_ref[...] = jnp.broadcast_to(both[None], partial_ref.shape)


def last_kernel(
    heads, hops, scale, gnorm_ref, scores_ref, keys_ref, ids_ref, parts_ref, *refs
):
    received = refs[:hops]
    value_grad_ref, threshold_grad_ref, gain_grad_ref = refs[hops:]
    rows, width = gnorm_ref.shape
    ids = ids_ref[...]
    returned = take_messages(received, tail_docs(ids))
    states = [returned[h * width : (h + 1) * width, :] for h in range(heads)]
    keys = keys_ref[...]
    across = pick_heads([dot_nn(keys, s) for s in states], last_rows(ids, heads, rows))
    value_grad_ref[...] = (dot_tn(scores_ref[...], gnorm_ref[...]) + across).astype(BF16)
    parts = parts_ref[...]
    even = lax.rem(row_iota(parts.shape), 2) == 0
    threshold_grad_ref[...] = jnp.sum(jnp.where(even, parts, 0.0), axis=0, keepdims=True) * scale
    gain_grad_ref[...] = jnp.sum(jnp.where(even, 0.0, parts), axis=0, keepdims=True) * scale


def call(kernel, name, out, *args):
    size = sum(a.size * a.dtype.itemsize for a in (*args, *out))
    return pl.pallas_call(
        kernel,
        name=name,
        out_shape=out,
        in_specs=[pl.BlockSpec(memory_space=pltpu.VMEM)] * len(args),
        out_specs=[pl.BlockSpec(memory_space=pltpu.VMEM)] * len(out),
        compiler_params=pltpu.CompilerParams(vmem_limit_bytes=VMEM_LIMIT),
        cost_estimate=pl.CostEstimate(flops=10**8, bytes_accessed=size, transcendentals=0),
    )(*args)


def shifted(x, by):
    count = lax.axis_size("ctx")
    pairs = [(i, i + by) for i in range(count) if 0 <= i + by < count]
    return lax.ppermute(x, "ctx", pairs)


def neighbours(message, reach, sign):
    if reach <= 3:
        return [shifted(message, sign * by) for by in range(1, reach + 1)]
    rows = message.shape[0] - MARK_ROWS
    state, marks = message[:rows], message[rows:]
    window = 1
    while window < reach:
        other = shifted(jnp.concatenate([state, marks]), sign * window)
        same = (other[rows:][:1] == marks[:1]).astype(F32)
        state = state + same * other[:rows]
        window = 2 * window
    return [shifted(jnp.concatenate([state, marks]), sign)]


def on_device(queries, spikes, values, threshold, norm_gain, document_ids, cotangent):
    length, heads, width = queries.shape
    rows = length * heads
    blocks = lax.axis_size("ctx")
    devices = blocks * lax.axis_size("head")
    reach = -(-(length * blocks // 4 - 1) // length)
    flat = lambda x: x.reshape(rows, width)
    q, s, v, ct = flat(queries), flat(spikes), flat(values), flat(cotangent)
    thr, gain, ids = threshold[None], norm_gain[None], document_ids[None]
    like = jax.ShapeDtypeStruct
    message = like((heads * width + MARK_ROWS, width), F32)

    (tail,) = call(functools.partial(tail_kernel, heads), "tail", [message], s, v, thr, ids)
    ahead = neighbours(tail, reach, 1)
    base, scores, mask, keys = call(
        functools.partial(inside_kernel, heads),
        "inside",
        [like((rows, width), F32), like((rows, rows), BF16), like((rows, rows), BF16),
         like((rows, width), BF16)],
        q, s, v, thr, ids,
    )
    attended, query_grad, gnorm, back, partial = call(
        functools.partial(middle_kernel, heads, len(ahead)),
        "middle",
        [like((rows, width), BF16), like((rows, width), BF16), like((rows, width), BF16),
         message, like((devices, 2, width), F32)],
        q, v, ct, base, mask, keys, thr, gain, ids, *ahead,
    )
    behind = neighbours(back, reach, -1)
    parts = lax.all_to_all(partial, ("ctx", "head"), 0, 0)
    scale = 1.0 / math.sqrt(rows * devices)
    value_grad, threshold_grad, gain_grad = call(
        functools.partial(last_kernel, heads, len(behind), scale),
        "last",
        [like((rows, width), BF16), like((1, width), F32), like((1, width), F32)],
        gnorm, scores, keys, ids, parts.reshape(2 * devices, width), *behind,
    )
    whole = lambda x: x.reshape(length, heads, width)
    return (
        whole(attended),
        whole(query_grad),
        whole(value_grad),
        threshold_grad[0],
        gain_grad[0],
    )


def solution(mesh):
    block = P("ctx", "head", None)
    return jax.shard_map(
        on_device,
        mesh=mesh,
        in_specs=(block, block, block, P(), P(), P("ctx"), block),
        out_specs=(block, block, block, P(), P()),
        check_vma=False,
    )
```

```python
import functools
import math

import jax
import jax.numpy as jnp
from jax import lax
from jax.experimental import pallas as pl
from jax.experimental.pallas import tpu as pltpu
from jax.sharding import PartitionSpec as P

BF16 = jnp.bfloat16
F32 = jnp.float32
MARK_ROWS = 8
VMEM_LIMIT = 48 * 1024 * 1024


def row_iota(shape):
    return lax.broadcasted_iota(jnp.int32, shape, 0)


def col_iota(shape):
    return lax.broadcasted_iota(jnp.int32, shape, 1)


def dot_nn(a, b):
    return lax.dot_general(a, b, (((1,), (0,)), ((), ())), preferred_element_type=F32)


def dot_nt(a, b):
    return lax.dot_general(a, b, (((1,), (1,)), ((), ())), preferred_element_type=F32)


def dot_tn(a, b):
    return lax.dot_general(a, b, (((0,), (0,)), ((), ())), preferred_element_type=F32)


def head_docs(ids):
    return ids[:, :1]


def tail_docs(ids):
    return ids[:, ids.shape[1] - 1 :]


def first_rows(ids, heads, rows):
    count = jnp.sum((ids == head_docs(ids)).astype(jnp.int32), axis=1, keepdims=True)
    return row_iota((rows, 1)) < heads * count


def last_rows(ids, heads, rows):
    count = jnp.sum((ids != tail_docs(ids)).astype(jnp.int32), axis=1, keepdims=True)
    return row_iota((rows, 1)) >= heads * count


def split_heads(x, keep, heads):
    head = lax.rem(row_iota((x.shape[0], 1)), heads)
    return jnp.concatenate(
        [jnp.where(keep & (head == h), x, jnp.zeros_like(x)) for h in range(heads)], axis=1
    )


def pick_heads(parts, keep):
    heads = len(parts)
    head = lax.rem(row_iota((parts[0].shape[0], 1)), heads)
    out = jnp.zeros_like(parts[0])
    for h in range(heads):
        out = jnp.where(keep & (head == h), parts[h], out)
    return out


def put_message(out_ref, state, mark):
    count = state.shape[0]
    out_ref[:count, :] = state
    out_ref[count:, :] = jnp.broadcast_to(mark.astype(F32), (MARK_ROWS, out_ref.shape[1]))


def take_messages(refs, mark):
    total = None
    for ref in refs:
        count = ref.shape[0] - MARK_ROWS
        same = (ref[count : count + 1, :] == mark.astype(F32)).astype(F32)
        part = ref[:count, :] * same
        total = part if total is None else total + part
    return total.astype(BF16)


def tail_kernel(heads, spikes_ref, values_ref, threshold_ref, ids_ref, tail_ref):
    ids = ids_ref[...]
    rows = values_ref.shape[0]
    keys = (spikes_ref[...].astype(F32) * threshold_ref[...]).astype(BF16)
    spread = split_heads(keys, last_rows(ids, heads, rows), heads)
    put_message(tail_ref, dot_tn(spread, values_ref[...]), tail_docs(ids))


def inside_kernel(
    heads, queries_ref, spikes_ref, values_ref, threshold_ref, ids_ref,
    base_ref, scores_ref, mask_ref, keys_ref,
):
    rows = queries_ref.shape[0]
    tokens = ids_ref.shape[1]
    queries = queries_ref[...]
    keys = (spikes_ref[...].astype(F32) * threshold_ref[...]).astype(BF16)
    keys_ref[...] = keys
    ids = ids_ref[...].astype(F32)
    apart = row_iota((rows, tokens)) - heads * col_iota((rows, tokens))
    down = jnp.sum(
        jnp.where((apart >= 0) & (apart < heads), ids, 0.0), axis=1, keepdims=True
    )
    r = row_iota((rows, rows))
    c = col_iota((rows, rows))
    across = jnp.sum(jnp.where(r == c, down, 0.0), axis=0, keepdims=True)
    allowed = (c <= r) & (down == across) & (lax.rem(r - c, heads) == 0)
    scores = jnp.where(allowed, dot_nt(queries, keys), 0.0).astype(BF16)
    scores_ref[...] = scores
    mask_ref[...] = allowed.astype(BF16)
    base_ref[...] = queries.astype(F32) + dot_nn(scores, values_ref[...])


def middle_kernel(
    heads, hops, queries_ref, values_ref, cotangent_ref, base_ref, mask_ref, keys_ref,
    threshold_ref, gain_ref, ids_ref, *refs,
):
    received = refs[:hops]
    attended_ref, query_grad_ref, gnorm_ref, back_ref, partial_ref = refs[hops:]
    rows, width = queries_ref.shape
    ids = ids_ref[...]
    queries = queries_ref[...]
    first = first_rows(ids, heads, rows)
    carried = take_messages(received, head_docs(ids))
    states = [carried[h * width : (h + 1) * width, :] for h in range(heads)]
    mixed = base_ref[...] + pick_heads([dot_nn(queries, s) for s in states], first)
    ratio = lax.rsqrt(jnp.mean(mixed * mixed, axis=1, keepdims=True) + 1e-06)
    normed = mixed * ratio
    gain = gain_ref[...]
    attended_ref[...] = (normed * gain).astype(BF16)
    cotangent = cotangent_ref[...].astype(F32)
    upstream = cotangent * gain
    inner = jnp.mean(normed * upstream, axis=1, keepdims=True)
    gnorm = (ratio * upstream - normed * ratio * inner).astype(BF16)
    gnorm_ref[...] = gnorm
    put_message(back_ref, dot_tn(split_heads(queries, first, heads), gnorm), head_docs(ids))
    dscores = (dot_nt(gnorm, values_ref[...]) * mask_ref[...].astype(F32)).astype(BF16)
    mixing = dot_nn(dscores, keys_ref[...])
    mixing = mixing + pick_heads([dot_nt(gnorm, s) for s in states], first)
    query_grad_ref[...] = (gnorm.astype(F32) + mixing).astype(BF16)
    threshold_part = (
        jnp.sum(queries.astype(F32) * mixing, axis=0, keepdims=True) / threshold_ref[...]
    )
    gain_part = jnp.sum(cotangent * normed, axis=0, keepdims=True)
    both = jnp.concatenate([threshold_part, gain_part], axis=0)
    partial_ref[...] = jnp.broadcast_to(both[None], partial_ref.shape)


def last_kernel(
    heads, hops, scale, gnorm_ref, scores_ref, keys_ref, ids_ref, parts_ref, *refs
):
    received = refs[:hops]
    value_grad_ref, threshold_grad_ref, gain_grad_ref = refs[hops:]
    rows, width = gnorm_ref.shape
    ids = ids_ref[...]
    returned = take_messages(received, tail_docs(ids))
    states = [returned[h * width : (h + 1) * width, :] for h in range(heads)]
    keys = keys_ref[...]
    across = pick_heads([dot_nn(keys, s) for s in states], last_rows(ids, heads, rows))
    value_grad_ref[...] = (dot_tn(scores_ref[...], gnorm_ref[...]) + across).astype(BF16)
    parts = parts_ref[...]
    even = lax.rem(row_iota(parts.shape), 2) == 0
    threshold_grad_ref[...] = jnp.sum(jnp.where(even, parts, 0.0), axis=0, keepdims=True) * scale
    gain_grad_ref[...] = jnp.sum(jnp.where(even, 0.0, parts), axis=0, keepdims=True) * scale


def call(kernel, name, out, *args):
    size = sum(a.size * a.dtype.itemsize for a in (*args, *out))
    return pl.pallas_call(
        kernel,
        name=name,
        out_shape=out,
        in_specs=[pl.BlockSpec(memory_space=pltpu.VMEM)] * len(args),
        out_specs=[pl.BlockSpec(memory_space=pltpu.VMEM)] * len(out),
        compiler_params=pltpu.CompilerParams(vmem_limit_bytes=VMEM_LIMIT),
        cost_estimate=pl.CostEstimate(flops=10**8, bytes_accessed=size, transcendentals=0),
    )(*args)


def shifted(x, by):
    count = lax.axis_size("ctx")
    pairs = [(i, (i + by) % count) for i in range(count)]
    return lax.ppermute(x, "ctx", pairs)


def neighbours(message, reach, sign):
    if reach <= 3:
        return [shifted(message, sign * by) for by in range(1, reach + 1)]
    rows = message.shape[0] - MARK_ROWS
    state, marks = message[:rows], message[rows:]
    window = 1
    while window < reach:
        other = shifted(jnp.concatenate([state, marks]), sign * window)
        same = (other[rows:][:1] == marks[:1]).astype(F32)
        state = state + same * other[:rows]
        window = 2 * window
    return [shifted(jnp.concatenate([state, marks]), sign)]


def on_device(queries, spikes, values, threshold, norm_gain, document_ids, cotangent):
    length, heads, width = queries.shape
    rows = length * heads
    blocks = lax.axis_size("ctx")
    devices = blocks * lax.axis_size("head")
    reach = -(-(length * blocks // 4 - 1) // length)
    flat = lambda x: x.reshape(rows, width)
    q, s, v, ct = flat(queries), flat(spikes), flat(values), flat(cotangent)
    thr, gain, ids = threshold[None], norm_gain[None], document_ids[None]
    like = jax.ShapeDtypeStruct
    message = like((heads * width + MARK_ROWS, width), F32)

    (tail,) = call(functools.partial(tail_kernel, heads), "tail", [message], s, v, thr, ids)
    ahead = neighbours(tail, reach, 1)
    base, scores, mask, keys = call(
        functools.partial(inside_kernel, heads),
        "inside",
        [like((rows, width), F32), like((rows, rows), BF16), like((rows, rows), BF16),
         like((rows, width), BF16)],
        q, s, v, thr, ids,
    )
    attended, query_grad, gnorm, back, partial = call(
        functools.partial(middle_kernel, heads, len(ahead)),
        "middle",
        [like((rows, width), BF16), like((rows, width), BF16), like((rows, width), BF16),
         message, like((devices, 2, width), F32)],
        q, v, ct, base, mask, keys, thr, gain, ids, *ahead,
    )
    behind = neighbours(back, reach, -1)
    parts = lax.all_to_all(partial, ("ctx", "head"), 0, 0)
    scale = 1.0 / math.sqrt(rows * devices)
    value_grad, threshold_grad, gain_grad = call(
        functools.partial(last_kernel, heads, len(behind), scale),
        "last",
        [like((rows, width), BF16), like((1, width), F32), like((1, width), F32)],
        gnorm, scores, keys, ids, parts.reshape(2 * devices, width), *behind,
    )
    whole = lambda x: x.reshape(length, heads, width)
    return (
        whole(attended),
        whole(query_grad),
        whole(value_grad),
        threshold_grad[0],
        gain_grad[0],
    )


def solution(mesh):
    block = P("ctx", "head", None)
    return jax.shard_map(
        on_device,
        mesh=mesh,
        in_specs=(block, block, block, P(), P(), P("ctx"), block),
        out_specs=(block, block, block, P(), P()),
        check_vma=False,
    )
```

```python
import functools
import math

import jax
import jax.numpy as jnp
from jax import lax
from jax.experimental import pallas as pl
from jax.experimental.pallas import tpu as pltpu
from jax.sharding import PartitionSpec as P

BF16 = jnp.bfloat16
F32 = jnp.float32
MARK_ROWS = 8
VMEM_LIMIT = 48 * 1024 * 1024


def row_iota(shape):
    return lax.broadcasted_iota(jnp.int32, shape, 0)


def col_iota(shape):
    return lax.broadcasted_iota(jnp.int32, shape, 1)


def dot_nn(a, b):
    return lax.dot_general(a, b, (((1,), (0,)), ((), ())), preferred_element_type=F32)


def dot_nt(a, b):
    return lax.dot_general(a, b, (((1,), (1,)), ((), ())), preferred_element_type=F32)


def dot_tn(a, b):
    return lax.dot_general(a, b, (((0,), (0,)), ((), ())), preferred_element_type=F32)


def head_docs(ids):
    return ids[:, :1]


def tail_docs(ids):
    return ids[:, ids.shape[1] - 1 :]


def first_rows(ids, heads, rows):
    count = jnp.sum((ids == head_docs(ids)).astype(jnp.int32), axis=1, keepdims=True)
    return row_iota((rows, 1)) < heads * count


def last_rows(ids, heads, rows):
    count = jnp.sum((ids != tail_docs(ids)).astype(jnp.int32), axis=1, keepdims=True)
    return row_iota((rows, 1)) >= heads * count


def spread_heads(x, keep, heads):
    head = lax.rem(row_iota((x.shape[0], 1)), heads)
    return jnp.concatenate(
        [jnp.where(keep & (head == h), x, jnp.zeros_like(x)) for h in range(heads)], axis=1
    )


def pick_heads(x, keep, heads):
    width = x.shape[1] // heads
    head = lax.rem(row_iota((x.shape[0], 1)), heads)
    out = jnp.zeros((x.shape[0], width), x.dtype)
    for h in range(heads):
        out = jnp.where(keep & (head == h), x[:, h * width : (h + 1) * width], out)
    return out


def put_message(out_ref, state, mark):
    count = state.shape[0]
    out_ref[:count, :] = state
    out_ref[count:, :] = jnp.broadcast_to(mark.astype(F32), (MARK_ROWS, out_ref.shape[1]))


def take_messages(refs, mark):
    total = None
    for ref in refs:
        count = ref.shape[0] - MARK_ROWS
        same = (ref[count : count + 1, :] == mark.astype(F32)).astype(F32)
        part = ref[:count, :] * same
        total = part if total is None else total + part
    return total.astype(BF16)


def pattern_kernel(heads, causal_ref, start_ref):
    r, c = row_iota(causal_ref.shape), col_iota(causal_ref.shape)
    causal_ref[...] = ((c <= r) & (lax.rem(r - c, heads) == 0)).astype(BF16)
    start_ref[...] = jnp.zeros_like(start_ref)


def tail_kernel(
    heads, spikes_ref, values_ref, threshold_ref, gain_ref, ids_ref, start_ref, tail_ref, keys_ref,
    gain_out_ref,
):
    gain_out_ref[...] = gain_ref[...]
    ids = ids_ref[...]
    rows = values_ref.shape[0]
    keys = (spikes_ref[...].astype(F32) * threshold_ref[...]).astype(BF16)
    keys_ref[...] = keys
    spread = spread_heads(values_ref[...], last_rows(ids, heads, rows), heads)
    put_message(tail_ref, dot_tn(keys, spread), tail_docs(ids))


def inside_kernel(
    heads, queries_ref, keys_ref, values_ref, ids_ref, causal_ref, base_ref, scores_ref, mask_ref
):
    rows = queries_ref.shape[0]
    tokens = ids_ref.shape[1]
    queries = queries_ref[...]
    ids = ids_ref[...].astype(F32)
    apart = row_iota((rows, tokens)) - heads * col_iota((rows, tokens))
    down = jnp.sum(
        jnp.where((apart >= 0) & (apart < heads), ids, 0.0), axis=1, keepdims=True
    )
    r = row_iota((rows, rows))
    c = col_iota((rows, rows))
    across = jnp.sum(jnp.where(r == c, down, 0.0), axis=0, keepdims=True)
    allowed = jnp.where(down == across, causal_ref[...].astype(F32), 0.0).astype(BF16)
    scores = dot_nt(queries, keys_ref[...]).astype(BF16) * allowed
    scores_ref[...] = scores
    mask_ref[...] = allowed
    base_ref[...] = queries.astype(F32) + dot_nn(scores, values_ref[...])


def middle_kernel(
    heads, hops, queries_ref, values_ref, cotangent_ref, base_ref, mask_ref, keys_ref,
    threshold_ref, gain_ref, ids_ref, *refs,
):
    received = refs[:hops]
    attended_ref, query_grad_ref, gnorm_ref, back_ref, partial_ref = refs[hops:]
    rows = queries_ref.shape[0]
    ids = ids_ref[...]
    queries = queries_ref[...]
    first = first_rows(ids, heads, rows)
    carried = take_messages(received, head_docs(ids))
    mixed = base_ref[...] + pick_heads(dot_nn(queries, carried), first, heads)
    ratio = lax.rsqrt(jnp.mean(mixed * mixed, axis=1, keepdims=True) + 1e-06)
    normed = mixed * ratio
    gain = gain_ref[...]
    attended_ref[...] = (normed * gain).astype(BF16)
    cotangent = cotangent_ref[...].astype(F32)
    upstream = cotangent * gain
    inner = jnp.mean(normed * upstream, axis=1, keepdims=True)
    gnorm = (ratio * upstream - normed * ratio * inner).astype(BF16)
    gnorm_ref[...] = gnorm
    spread = spread_heads(gnorm, first, heads)
    put_message(back_ref, dot_tn(queries, spread), head_docs(ids))
    dscores = dot_nt(gnorm, values_ref[...]).astype(BF16) * mask_ref[...]
    mixing = dot_nn(dscores, keys_ref[...]) + dot_nt(spread, carried)
    query_grad_ref[...] = (gnorm.astype(F32) + mixing).astype(BF16)
    threshold_part = (
        jnp.sum(queries.astype(F32) * mixing, axis=0, keepdims=True) / threshold_ref[...]
    )
    gain_part = jnp.sum(cotangent * normed, axis=0, keepdims=True)
    both = jnp.concatenate([threshold_part, gain_part], axis=0)
    partial_ref[...] = jnp.broadcast_to(both[None], partial_ref.shape)


def last_kernel(
    heads, hops, scale, gnorm_ref, scores_ref, keys_ref, ids_ref, parts_ref,
    attended_ref, query_grad_ref, *refs,
):
    received = refs[:hops]
    attended_hbm, query_grad_hbm, value_grad_hbm, threshold_hbm, gain_hbm = refs[hops : hops + 5]
    value_grad_ref, threshold_ref, gain_ref, sems = refs[hops + 5 :]
    copies = [
        pltpu.make_async_copy(attended_ref, attended_hbm, sems.at[0]),
        pltpu.make_async_copy(query_grad_ref, query_grad_hbm, sems.at[1]),
        pltpu.make_async_copy(value_grad_ref, value_grad_hbm, sems.at[2]),
        pltpu.make_async_copy(threshold_ref, threshold_hbm, sems.at[3]),
        pltpu.make_async_copy(gain_ref, gain_hbm, sems.at[4]),
    ]
    copies[0].start()
    copies[1].start()
    parts = parts_ref[...]
    even = lax.rem(row_iota(parts.shape), 2) == 0
    threshold_ref[...] = jnp.sum(jnp.where(even, parts, 0.0), axis=0, keepdims=True) * scale
    copies[3].start()
    gain_ref[...] = jnp.sum(jnp.where(even, 0.0, parts), axis=0, keepdims=True) * scale
    copies[4].start()
    ids = ids_ref[...]
    rows = gnorm_ref.shape[0]
    returned = take_messages(received, tail_docs(ids))
    across = pick_heads(dot_nn(keys_ref[...], returned), last_rows(ids, heads, rows), heads)
    value_grad_ref[...] = (dot_tn(scores_ref[...], gnorm_ref[...]) + across).astype(BF16)
    copies[2].start()
    for copy in copies:
        copy.wait()


VMEM = pl.BlockSpec(memory_space=pltpu.VMEM)
HBM = pl.BlockSpec(memory_space=pltpu.HBM)


def call(kernel, name, out, args, in_space=VMEM, out_spaces=None, scratch=(), flops=10**8):
    size = sum(a.size * a.dtype.itemsize for a in (*args, *out))
    return pl.pallas_call(
        kernel,
        name=name,
        out_shape=out,
        in_specs=[in_space] * len(args),
        out_specs=out_spaces or [VMEM] * len(out),
        scratch_shapes=list(scratch),
        compiler_params=pltpu.CompilerParams(vmem_limit_bytes=VMEM_LIMIT),
        cost_estimate=pl.CostEstimate(flops=flops, bytes_accessed=size, transcendentals=0),
    )(*args)


def shifted(x, by):
    count = lax.axis_size("ctx")
    pairs = [(i, (i + by) % count) for i in range(count)]
    return lax.ppermute(x, "ctx", pairs)


def neighbours(message, reach, sign):
    if reach <= 3:
        return [shifted(message, sign * by) for by in range(1, reach + 1)]
    rows = message.shape[0] - MARK_ROWS
    state, marks = message[:rows], message[rows:]
    window = 1
    while window < reach:
        other = shifted(jnp.concatenate([state, marks]), sign * window)
        same = (other[rows:][:1] == marks[:1]).astype(F32)
        state = state + same * other[:rows]
        window = 2 * window
    return [shifted(jnp.concatenate([state, marks]), sign)]


def on_device(queries, spikes, values, threshold, norm_gain, document_ids, cotangent):
    length, heads, width = queries.shape
    rows = length * heads
    blocks = lax.axis_size("ctx")
    devices = blocks * lax.axis_size("head")
    reach = -(-(length * blocks // 4 - 1) // length)
    flat = lambda x: x.reshape(rows, width)
    q, s, v, ct = flat(queries), flat(spikes), flat(values), flat(cotangent)
    thr, gain, ids = threshold[None], norm_gain[None], document_ids[None]
    like = jax.ShapeDtypeStruct
    message = like((width + MARK_ROWS, heads * width), F32)
    flat_bf = like((rows, width), BF16)
    row_f = like((1, width), F32)

    causal, start = call(
        functools.partial(pattern_kernel, heads),
        "pattern",
        [like((rows, rows), BF16), like((8, 128), F32)],
        (),
        flops=4 * 10**9,
    )
    tail, keys, gain = call(
        functools.partial(tail_kernel, heads),
        "tail",
        [message, flat_bf, row_f],
        (s, v, thr, gain, ids, start),
    )
    ahead = neighbours(tail, reach, 1)
    base, scores, mask = call(
        functools.partial(inside_kernel, heads),
        "inside",
        [like((rows, width), F32), like((rows, rows), BF16), like((rows, rows), BF16)],
        (q, keys, v, ids, causal),
    )
    attended, query_grad, gnorm, back, partial = call(
        functools.partial(middle_kernel, heads, len(ahead)),
        "middle",
        [flat_bf, flat_bf, flat_bf, message, like((devices, 2, width), F32)],
        (q, v, ct, base, mask, keys, thr, gain, ids, *ahead),
    )
    behind = neighbours(back, reach, -1)
    parts = lax.all_to_all(partial, ("ctx", "head"), 0, 0)
    scale = 1.0 / math.sqrt(rows * devices)
    attended, query_grad, value_grad, threshold_grad, gain_grad = call(
        functools.partial(last_kernel, heads, len(behind), scale),
        "last",
        [flat_bf, flat_bf, flat_bf, row_f, row_f],
        (gnorm, scores, keys, ids, parts.reshape(2 * devices, width), attended, query_grad,
         *behind),
        out_spaces=[HBM] * 5,
        scratch=[pltpu.VMEM((rows, width), BF16), pltpu.VMEM((1, width), F32),
                 pltpu.VMEM((1, width), F32), pltpu.SemaphoreType.DMA((5,))],
    )
    whole = lambda x: x.reshape(length, heads, width)
    return (
        whole(attended),
        whole(query_grad),
        whole(value_grad),
        threshold_grad[0],
        gain_grad[0],
    )


def solution(mesh):
    block = P("ctx", "head", None)
    return jax.shard_map(
        on_device,
        mesh=mesh,
        in_specs=(block, block, block, P(), P(), P("ctx"), block),
        out_specs=(block, block, block, P(), P()),
        check_vma=False,
    )
```

```python
import functools
import math

import jax
import jax.numpy as jnp
from jax import lax
from jax.experimental import pallas as pl
from jax.experimental.pallas import tpu as pltpu
from jax.sharding import PartitionSpec as P

BF16 = jnp.bfloat16
F32 = jnp.float32
MARK_ROWS = 8
VMEM_LIMIT = 48 * 1024 * 1024


def row_iota(shape):
    return lax.broadcasted_iota(jnp.int32, shape, 0)


def col_iota(shape):
    return lax.broadcasted_iota(jnp.int32, shape, 1)


def dot_nn(a, b):
    return lax.dot_general(a, b, (((1,), (0,)), ((), ())), preferred_element_type=F32)


def dot_nt(a, b):
    return lax.dot_general(a, b, (((1,), (1,)), ((), ())), preferred_element_type=F32)


def dot_tn(a, b):
    return lax.dot_general(a, b, (((0,), (0,)), ((), ())), preferred_element_type=F32)


def spread_heads(x, own_ref):
    return jnp.concatenate([x * own_ref[h] for h in range(own_ref.shape[0])], axis=1)


def pick_heads(x, keep, own_ref):
    heads, _, width = own_ref.shape
    out = x[:, :width]
    for h in range(1, heads):
        out = jnp.where(own_ref[h] > 0, x[:, h * width : (h + 1) * width], out)
    return out * keep


def put_message(out_ref, state, mark_ref):
    count = state.shape[0]
    out_ref[:count, :] = state
    out_ref[count:, :] = mark_ref[...]


def take_messages(refs, mark_ref):
    total = None
    for ref in refs:
        count = ref.shape[0] - MARK_ROWS
        same = (ref[count : count + 1, :] == mark_ref[:1, :]).astype(F32)
        part = ref[:count, :] * same
        total = part if total is None else total + part
    return total.astype(BF16)


def pattern_kernel(heads, own_ref):
    head = lax.rem(row_iota(own_ref.shape[1:]), heads)
    for h in range(heads):
        own_ref[h] = (head == h).astype(BF16)


def marks_kernel(
    heads, ids_ref, threshold_ref, first_ref, last_ref, head_mark_ref, tail_mark_ref, threshold_out_ref
):
    threshold_out_ref[...] = threshold_ref[...]
    ids = ids_ref[...]
    head, tail = ids[:, :1], ids[:, ids.shape[1] - 1 :]
    in_first = jnp.sum((ids == head).astype(jnp.int32), axis=1, keepdims=True)
    before_last = jnp.sum((ids != tail).astype(jnp.int32), axis=1, keepdims=True)
    row = row_iota(first_ref.shape)
    first_ref[...] = (row < heads * in_first).astype(F32)
    last_ref[...] = (row >= heads * before_last).astype(F32)
    head_mark_ref[...] = jnp.broadcast_to(head.astype(F32), head_mark_ref.shape)
    tail_mark_ref[...] = jnp.broadcast_to(tail.astype(F32), tail_mark_ref.shape)


def tail_kernel(
    heads, spikes_ref, values_ref, threshold_ref, last_ref, tail_mark_ref, own_ref, tail_ref, keys_ref
):
    keys = spikes_ref[...].astype(F32) * threshold_ref[...]
    keys_ref[...] = keys.astype(BF16)
    kept = (keys * last_ref[...]).astype(BF16)
    put_message(tail_ref, dot_tn(kept, spread_heads(values_ref[...], own_ref)), tail_mark_ref)


def inside_kernel(
    heads, queries_ref, keys_ref, values_ref, cotangent_ref, gain_ref, ids_ref,
    base_ref, scores_t_ref, mask_ref, queries_t_ref, values_t_ref, own_ref, upstream_ref, gain_out_ref,
):
    rows = queries_ref.shape[0]
    tokens = ids_ref.shape[1]
    queries = queries_ref[...]
    ids = ids_ref[...].astype(F32)
    apart = row_iota((rows, tokens)) - heads * col_iota((rows, tokens))
    down = jnp.sum(
        jnp.where((apart >= 0) & (apart < heads), ids, 0.0), axis=1, keepdims=True
    )
    r = row_iota((rows, rows))
    c = col_iota((rows, rows))
    across = jnp.sum(jnp.where(r == c, down, 0.0), axis=0, keepdims=True)
    together = (down == across) & (lax.rem(r - c, heads) == 0)
    allowed = (together & (c <= r)).astype(F32).astype(BF16)
    allowed_t = (together & (r <= c)).astype(F32).astype(BF16)
    keys = keys_ref[...]
    scores = dot_nt(queries, keys).astype(BF16) * allowed
    scores_t_ref[...] = dot_nt(keys, queries).astype(BF16) * allowed_t
    mask_ref[...] = allowed
    queries_t_ref[...] = queries.T
    values_t_ref[...] = values_ref[...].T
    head = lax.rem(row_iota(own_ref.shape[1:]), heads)
    for h in range(heads):
        own_ref[h] = (head == h).astype(F32)
    gain_out_ref[...] = gain_ref[...]
    upstream_ref[...] = cotangent_ref[...].astype(F32) * gain_ref[...]
    base_ref[...] = queries.astype(F32) + dot_nn(scores, values_ref[...])


def middle_kernel(
    heads, hops, queries_ref, queries_t_ref, values_t_ref, cotangent_ref, upstream_ref, base_ref, mask_ref, keys_ref,
    threshold_ref, gain_ref, first_ref, head_mark_ref, own_ref, own_f_ref, *refs,
):
    received = refs[:hops]
    attended_ref, query_grad_ref, gnorm_ref, back_ref, partial_ref = refs[hops:]
    rows, width = queries_ref.shape
    carried = take_messages(received, head_mark_ref)
    gain = gain_ref[...]
    first = first_ref[...]
    queries = queries_ref[...]
    mixed = base_ref[...] + pick_heads(dot_nn(queries, carried), first, own_f_ref)
    cotangent = cotangent_ref[...].astype(F32)
    upstream = upstream_ref[...]
    square = jnp.mean(mixed * mixed, axis=1, keepdims=True)
    inner = jnp.mean(mixed * upstream, axis=1, keepdims=True)
    ratio = lax.rsqrt(square + 1e-06)
    gnorm_f = ratio * upstream - mixed * (ratio * ratio * ratio * inner)
    gnorm = gnorm_f.astype(BF16)
    gnorm_ref[...] = gnorm
    spread = spread_heads((gnorm_f * first).astype(BF16), own_ref)
    half = rows // 2
    early = dot_nn(gnorm[:half], values_t_ref[:, :half]).astype(BF16) * mask_ref[:half, :half]
    late = dot_nn(gnorm[half:], values_t_ref[...]).astype(BF16) * mask_ref[half:, :]
    mixing = jnp.concatenate(
        [dot_nn(early, keys_ref[:half, :]), dot_nn(late, keys_ref[...])], axis=0
    ) + dot_nt(spread, carried)
    query_grad_ref[...] = (gnorm.astype(F32) + mixing).astype(BF16)
    normed = mixed * ratio
    attended_ref[...] = (normed * gain).astype(BF16)
    gain_sum = jnp.sum(cotangent * normed, axis=0, keepdims=True)
    threshold_sum = jnp.sum(queries.astype(F32) * mixing, axis=0, keepdims=True)
    put_message(back_ref, dot_nn(queries_t_ref[...], spread), head_mark_ref)
    both = jnp.concatenate([threshold_sum / threshold_ref[...], gain_sum], axis=0)
    partial_ref[...] = jnp.broadcast_to(both[None], partial_ref.shape)


def last_kernel(
    heads, hops, scale, gnorm_ref, scores_t_ref, keys_ref, last_ref, tail_mark_ref, own_f_ref, parts_ref,
    attended_ref, query_grad_ref, *refs,
):
    received = refs[:hops]
    attended_hbm, query_grad_hbm, value_grad_hbm, threshold_hbm, gain_hbm = refs[hops : hops + 5]
    value_grad_ref, threshold_ref, gain_ref, sems = refs[hops + 5 :]
    copies = [
        pltpu.make_async_copy(attended_ref, attended_hbm, sems.at[0]),
        pltpu.make_async_copy(query_grad_ref, query_grad_hbm, sems.at[1]),
        pltpu.make_async_copy(value_grad_ref, value_grad_hbm, sems.at[2]),
        pltpu.make_async_copy(threshold_ref, threshold_hbm, sems.at[3]),
        pltpu.make_async_copy(gain_ref, gain_hbm, sems.at[4]),
    ]
    copies[0].start()
    copies[1].start()
    parts = parts_ref[...]
    even = lax.rem(row_iota(parts.shape), 2) == 0
    threshold_ref[...] = jnp.sum(jnp.where(even, parts, 0.0), axis=0, keepdims=True) * scale
    copies[3].start()
    gain_ref[...] = jnp.sum(jnp.where(even, 0.0, parts), axis=0, keepdims=True) * scale
    copies[4].start()
    returned = take_messages(received, tail_mark_ref)
    across = pick_heads(dot_nn(keys_ref[...], returned), last_ref[...], own_f_ref)
    value_grad_ref[...] = (dot_nn(scores_t_ref[...], gnorm_ref[...]) + across).astype(BF16)
    copies[2].start()
    for copy in copies:
        copy.wait()


VMEM = pl.BlockSpec(memory_space=pltpu.VMEM)
HBM = pl.BlockSpec(memory_space=pltpu.HBM)


def call(
    kernel, name, out, args, in_space=VMEM, out_spaces=None, scratch=(), flops=10**8, size=None
):
    if size is None:
        size = sum(a.size * a.dtype.itemsize for a in (*args, *out))
    return pl.pallas_call(
        kernel,
        name=name,
        out_shape=out,
        in_specs=[in_space] * len(args),
        out_specs=out_spaces or [VMEM] * len(out),
        scratch_shapes=list(scratch),
        compiler_params=pltpu.CompilerParams(vmem_limit_bytes=VMEM_LIMIT),
        cost_estimate=pl.CostEstimate(flops=flops, bytes_accessed=size, transcendentals=0),
    )(*args)


def shifted(x, by):
    count = lax.axis_size("ctx")
    pairs = [(i, (i + by) % count) for i in range(count)]
    return lax.ppermute(x, "ctx", pairs)


def neighbours(message, reach, sign):
    if reach <= 3:
        return [shifted(message, sign * by) for by in range(1, reach + 1)]
    rows = message.shape[0] - MARK_ROWS
    state, marks = message[:rows], message[rows:]
    window = 1
    while window < reach:
        other = shifted(jnp.concatenate([state, marks]), sign * window)
        same = (other[rows:][:1] == marks[:1]).astype(F32)
        state = state + same * other[:rows]
        window = 2 * window
    return [shifted(jnp.concatenate([state, marks]), sign)]


def on_device(queries, spikes, values, threshold, norm_gain, document_ids, cotangent):
    length, heads, width = queries.shape
    rows = length * heads
    blocks = lax.axis_size("ctx")
    devices = blocks * lax.axis_size("head")
    reach = -(-(length * blocks // 4 - 1) // length)
    flat = lambda x: x.reshape(rows, width)
    q, s, v, ct = flat(queries), flat(spikes), flat(values), flat(cotangent)
    thr, gain, ids = threshold[None], norm_gain[None], document_ids[None]
    like = jax.ShapeDtypeStruct
    message = like((width + MARK_ROWS, heads * width), F32)
    flat_bf = like((rows, width), BF16)
    row_f = like((1, width), F32)

    flat_f = like((rows, width), F32)
    square = like((rows, rows), BF16)
    turned = like((width, rows), BF16)
    (own,) = call(
        functools.partial(pattern_kernel, heads),
        "pattern",
        [like((heads, rows, width), BF16)],
        (),
        flops=4 * 10**9,
    )
    mark = like((MARK_ROWS, heads * width), F32)
    first, last, head_mark, tail_mark, thr = call(
        functools.partial(marks_kernel, heads), "marks", [flat_f, flat_f, mark, mark, row_f], (ids, thr),
        flops=1, size=1,
    )
    tail, keys = call(
        functools.partial(tail_kernel, heads),
        "tail",
        [message, flat_bf],
        (s, v, thr, last, tail_mark, own),
    )
    ahead = neighbours(tail, reach, 1)
    base, scores_t, mask, q_t, v_t, own_f, upstream, gain = call(
        functools.partial(inside_kernel, heads),
        "inside",
        [flat_f, square, square, turned, turned, like((heads, rows, width), F32), flat_f, row_f],
        (q, keys, v, ct, gain, ids),
    )
    attended, query_grad, gnorm, back, partial = call(
        functools.partial(middle_kernel, heads, len(ahead)),
        "middle",
        [flat_bf, flat_bf, flat_bf, message, like((devices, 2, width), F32)],
        (q, q_t, v_t, ct, upstream, base, mask, keys, thr, gain, first, head_mark, own, own_f, *ahead),
    )
    behind = neighbours(back, reach, -1)
    parts = lax.all_to_all(partial, ("ctx", "head"), 0, 0)
    scale = 1.0 / math.sqrt(rows * devices)
    attended, query_grad, value_grad, threshold_grad, gain_grad = call(
        functools.partial(last_kernel, heads, len(behind), scale),
        "last",
        [flat_bf, flat_bf, flat_bf, row_f, row_f],
        (gnorm, scores_t, keys, last, tail_mark, own_f, parts.reshape(2 * devices, width), attended, query_grad,
         *behind),
        out_spaces=[HBM] * 5,
        scratch=[pltpu.VMEM((rows, width), BF16), pltpu.VMEM((1, width), F32),
                 pltpu.VMEM((1, width), F32), pltpu.SemaphoreType.DMA((5,))],
    )
    whole = lambda x: x.reshape(length, heads, width)
    return (
        whole(attended),
        whole(query_grad),
        whole(value_grad),
        threshold_grad[0],
        gain_grad[0],
    )


def solution(mesh):
    block = P("ctx", "head", None)
    return jax.shard_map(
        on_device,
        mesh=mesh,
        in_specs=(block, block, block, P(), P(), P("ctx"), block),
        out_specs=(block, block, block, P(), P()),
        check_vma=False,
    )
```

```python
import functools
import math

import jax
import jax.numpy as jnp
from jax import lax
from jax.experimental import pallas as pl
from jax.experimental.pallas import tpu as pltpu
from jax.sharding import PartitionSpec as P

BF16 = jnp.bfloat16
F32 = jnp.float32
MARK_ROWS = 8
VMEM_LIMIT = 48 * 1024 * 1024


def row_iota(shape):
    return lax.broadcasted_iota(jnp.int32, shape, 0)


def col_iota(shape):
    return lax.broadcasted_iota(jnp.int32, shape, 1)


def dot_nn(a, b):
    return lax.dot_general(a, b, (((1,), (0,)), ((), ())), preferred_element_type=F32)


def dot_nt(a, b):
    return lax.dot_general(a, b, (((1,), (1,)), ((), ())), preferred_element_type=F32)


def dot_tn(a, b):
    return lax.dot_general(a, b, (((0,), (0,)), ((), ())), preferred_element_type=F32)


def spread_heads(x, own_ref):
    return jnp.concatenate([x * own_ref[h] for h in range(own_ref.shape[0])], axis=1)


def put_message(out_ref, state, mark_ref):
    count, width = state.shape[0], out_ref.shape[1]
    for h in range(state.shape[1] // width):
        out_ref[h * count : (h + 1) * count, :] = state[:, h * width : (h + 1) * width]
    out_ref[out_ref.shape[0] - MARK_ROWS :, :] = mark_ref[...]


def take_messages(refs, mark_ref):
    total = None
    for ref in refs:
        count = ref.shape[0] - MARK_ROWS
        same = (ref[count : count + 1, :] == mark_ref[:1, :]).astype(F32)
        part = ref[:count, :] * same
        total = part if total is None else total + part
    return total.astype(BF16)


def side_by_side(state, heads):
    count = state.shape[0] // heads
    return jnp.concatenate([state[h * count : (h + 1) * count] for h in range(heads)], axis=1)


def pattern_kernel(heads, own_ref):
    head = lax.rem(row_iota(own_ref.shape[1:]), heads)
    for h in range(heads):
        own_ref[h] = (head == h).astype(BF16)


def marks_kernel(
    heads, ids_ref, threshold_ref, last_ref, tail_mark_ref, threshold_out_ref
):
    threshold_out_ref[...] = threshold_ref[...]
    ids = ids_ref[...]
    tail = ids[:, ids.shape[1] - 1 :]
    before_last = jnp.sum((ids != tail).astype(jnp.int32), axis=1, keepdims=True)
    last_ref[...] = (row_iota(last_ref.shape) >= heads * before_last).astype(F32)
    tail_mark_ref[...] = jnp.broadcast_to(tail.astype(F32), tail_mark_ref.shape)


def tail_kernel(
    heads, spikes_ref, values_ref, threshold_ref, last_ref, tail_mark_ref, own_ref, tail_ref, keys_ref
):
    keys = spikes_ref[...].astype(F32) * threshold_ref[...]
    keys_ref[...] = keys.astype(BF16)
    kept = (keys * last_ref[...]).astype(BF16)
    put_message(tail_ref, dot_tn(kept, spread_heads(values_ref[...], own_ref)), tail_mark_ref)


def inside_kernel(
    heads, queries_ref, keys_ref, values_ref, cotangent_ref, gain_ref, ids_ref, last_ref, own_ref,
    first_ref, head_mark_ref, base_ref, scores_t_ref, mask_ref, values_t_ref, first_queries_ref,
    first_queries_t_ref, last_keys_ref, upstream_ref, gain_out_ref,
):
    rows = queries_ref.shape[0]
    tokens = ids_ref.shape[1]
    queries = queries_ref[...]
    ids = ids_ref[...].astype(F32)
    head = ids[:, :1]
    in_first = jnp.sum((ids == head).astype(jnp.int32), axis=1, keepdims=True)
    first = (row_iota(first_ref.shape) < heads * in_first).astype(F32)
    first_ref[...] = first
    head_mark_ref[...] = jnp.broadcast_to(head, head_mark_ref.shape)
    apart = row_iota((rows, tokens)) - heads * col_iota((rows, tokens))
    down = jnp.sum(
        jnp.where((apart >= 0) & (apart < heads), ids, 0.0), axis=1, keepdims=True
    )
    r = row_iota((rows, rows))
    c = col_iota((rows, rows))
    across = jnp.sum(jnp.where(r == c, down, 0.0), axis=0, keepdims=True)
    together = (down == across) & (lax.rem(r - c, heads) == 0)
    allowed = (together & (c <= r)).astype(F32).astype(BF16)
    allowed_t = (together & (r <= c)).astype(F32).astype(BF16)
    keys = keys_ref[...]
    scores = dot_nt(queries, keys).astype(BF16) * allowed
    scores_t_ref[...] = dot_nt(keys, queries).astype(BF16) * allowed_t
    mask_ref[...] = allowed
    values_t_ref[...] = values_ref[...].T
    first_queries = spread_heads(
        (queries.astype(F32) * first).astype(BF16), own_ref
    )
    first_queries_ref[...] = first_queries
    first_queries_t_ref[...] = first_queries.T
    last_keys_ref[...] = spread_heads((keys.astype(F32) * last_ref[...]).astype(BF16), own_ref)
    gain_out_ref[...] = gain_ref[...]
    upstream_ref[...] = cotangent_ref[...].astype(F32) * gain_ref[...]
    base_ref[...] = queries.astype(F32) + dot_nn(scores, values_ref[...])


def middle_kernel(
    heads, hops, queries_ref, first_queries_ref, first_queries_t_ref, values_t_ref, cotangent_ref,
    upstream_ref, base_ref, mask_ref, keys_ref, threshold_ref, gain_ref, first_ref, head_mark_ref,
    own_ref, *refs,
):
    received = refs[:hops]
    attended_ref, query_grad_ref, gnorm_ref, back_ref, partial_ref = refs[hops:]
    rows, width = queries_ref.shape
    carried = take_messages(received, head_mark_ref)
    gain = gain_ref[...]
    first = first_ref[...]
    queries = queries_ref[...]
    mixed = base_ref[...] + dot_nn(first_queries_ref[...], carried)
    cotangent = cotangent_ref[...].astype(F32)
    upstream = upstream_ref[...]
    square = jnp.mean(mixed * mixed, axis=1, keepdims=True)
    inner = jnp.mean(mixed * upstream, axis=1, keepdims=True)
    ratio = lax.rsqrt(square + 1e-06)
    gnorm_f = ratio * upstream - mixed * (ratio * ratio * ratio * inner)
    gnorm = gnorm_f.astype(BF16)
    gnorm_ref[...] = gnorm
    spread = spread_heads((gnorm_f * first).astype(BF16), own_ref)
    half = rows // 2
    early = dot_nn(gnorm[:half], values_t_ref[:, :half]).astype(BF16) * mask_ref[:half, :half]
    late = dot_nn(gnorm[half:], values_t_ref[...]).astype(BF16) * mask_ref[half:, :]
    mixing = jnp.concatenate(
        [dot_nn(early, keys_ref[:half, :]), dot_nn(late, keys_ref[...])], axis=0
    ) + dot_nt(spread, side_by_side(carried, heads))
    query_grad_ref[...] = (gnorm.astype(F32) + mixing).astype(BF16)
    normed = mixed * ratio
    attended_ref[...] = (normed * gain).astype(BF16)
    gain_sum = jnp.sum(cotangent * normed, axis=0, keepdims=True)
    threshold_sum = jnp.sum(queries.astype(F32) * mixing, axis=0, keepdims=True)
    put_message(back_ref, dot_nn(first_queries_t_ref[...], gnorm), head_mark_ref)
    both = jnp.concatenate([threshold_sum / threshold_ref[...], gain_sum], axis=0)
    partial_ref[...] = jnp.broadcast_to(both[None], partial_ref.shape)


def last_kernel(
    heads, hops, scale, gnorm_ref, scores_t_ref, last_keys_ref, tail_mark_ref, parts_ref,
    attended_ref, query_grad_ref, *refs,
):
    received = refs[:hops]
    attended_hbm, query_grad_hbm, value_grad_hbm, threshold_hbm, gain_hbm = refs[hops : hops + 5]
    value_grad_ref, threshold_ref, gain_ref, sems = refs[hops + 5 :]
    copies = [
        pltpu.make_async_copy(attended_ref, attended_hbm, sems.at[0]),
        pltpu.make_async_copy(query_grad_ref, query_grad_hbm, sems.at[1]),
        pltpu.make_async_copy(value_grad_ref, value_grad_hbm, sems.at[2]),
        pltpu.make_async_copy(threshold_ref, threshold_hbm, sems.at[3]),
        pltpu.make_async_copy(gain_ref, gain_hbm, sems.at[4]),
    ]
    copies[0].start()
    copies[1].start()
    parts = parts_ref[...]
    even = lax.rem(row_iota(parts.shape), 2) == 0
    threshold_ref[...] = jnp.sum(jnp.where(even, parts, 0.0), axis=0, keepdims=True) * scale
    copies[3].start()
    gain_ref[...] = jnp.sum(jnp.where(even, 0.0, parts), axis=0, keepdims=True) * scale
    copies[4].start()
    returned = take_messages(received, tail_mark_ref)
    across = dot_nn(last_keys_ref[...], returned)
    value_grad_ref[...] = (dot_nn(scores_t_ref[...], gnorm_ref[...]) + across).astype(BF16)
    copies[2].start()
    for copy in copies:
        copy.wait()


VMEM = pl.BlockSpec(memory_space=pltpu.VMEM)
HBM = pl.BlockSpec(memory_space=pltpu.HBM)


def call(
    kernel, name, out, args, in_space=VMEM, out_spaces=None, scratch=(), flops=10**8, size=None
):
    if size is None:
        size = sum(a.size * a.dtype.itemsize for a in (*args, *out))
    return pl.pallas_call(
        kernel,
        name=name,
        out_shape=out,
        in_specs=[in_space] * len(args),
        out_specs=out_spaces or [VMEM] * len(out),
        scratch_shapes=list(scratch),
        compiler_params=pltpu.CompilerParams(vmem_limit_bytes=VMEM_LIMIT),
        cost_estimate=pl.CostEstimate(flops=flops, bytes_accessed=size, transcendentals=0),
    )(*args)


def shifted(x, by):
    count = lax.axis_size("ctx")
    pairs = [(i, (i + by) % count) for i in range(count)]
    return lax.ppermute(x, "ctx", pairs)


def neighbours(message, reach, sign):
    if reach <= 3:
        order = range(reach, 0, -1) if sign > 0 else range(1, reach + 1)
        return [shifted(message, sign * by) for by in order]
    rows = message.shape[0] - MARK_ROWS
    state, marks = message[:rows], message[rows:]
    window = 1
    while window < reach:
        other = shifted(jnp.concatenate([state, marks]), sign * window)
        same = (other[rows:][:1] == marks[:1]).astype(F32)
        state = state + same * other[:rows]
        window = 2 * window
    return [shifted(jnp.concatenate([state, marks]), sign)]


def on_device(queries, spikes, values, threshold, norm_gain, document_ids, cotangent):
    length, heads, width = queries.shape
    rows = length * heads
    blocks = lax.axis_size("ctx")
    devices = blocks * lax.axis_size("head")
    reach = -(-(length * blocks // 4 - 1) // length)
    flat = lambda x: x.reshape(rows, width)
    q, s, v, ct = flat(queries), flat(spikes), flat(values), flat(cotangent)
    thr, gain, ids = threshold[None], norm_gain[None], document_ids[None]
    like = jax.ShapeDtypeStruct
    message = like((heads * width + MARK_ROWS, width), F32)
    flat_bf = like((rows, width), BF16)
    row_f = like((1, width), F32)

    flat_f = like((rows, width), F32)
    square = like((rows, rows), BF16)
    (own,) = call(
        functools.partial(pattern_kernel, heads),
        "pattern",
        [like((heads, rows, width), BF16)],
        (),
        flops=4 * 10**9,
    )
    mark = like((MARK_ROWS, width), F32)
    last, tail_mark, thr = call(
        functools.partial(marks_kernel, heads), "marks", [flat_f, mark, row_f], (ids, thr),
        flops=1, size=1,
    )
    tail, keys = call(
        functools.partial(tail_kernel, heads),
        "tail",
        [message, flat_bf],
        (s, v, thr, last, tail_mark, own),
    )
    ahead = neighbours(tail, reach, 1)
    wide = like((rows, heads * width), BF16)
    first, head_mark, base, scores_t, mask, v_t, first_q, first_q_t, last_k, upstream, gain = call(
        functools.partial(inside_kernel, heads),
        "inside",
        [flat_f, mark, flat_f, square, square, like((width, rows), BF16), wide, like((heads * width, rows), BF16),
         wide, flat_f, row_f],
        (q, keys, v, ct, gain, ids, last, own),
    )
    attended, query_grad, gnorm, back, partial = call(
        functools.partial(middle_kernel, heads, len(ahead)),
        "middle",
        [flat_bf, flat_bf, flat_bf, message, like((devices, 2, width), F32)],
        (q, first_q, first_q_t, v_t, ct, upstream, base, mask, keys, thr, gain, first, head_mark, own,
         *ahead),
    )
    behind = neighbours(back, reach, -1)
    parts = lax.all_to_all(partial, ("head", "ctx"), 0, 0)
    scale = 1.0 / math.sqrt(rows * devices)
    attended, query_grad, value_grad, threshold_grad, gain_grad = call(
        functools.partial(last_kernel, heads, len(behind), scale),
        "last",
        [flat_bf, flat_bf, flat_bf, row_f, row_f],
        (gnorm, scores_t, last_k, tail_mark, parts.reshape(2 * devices, width), attended, query_grad,
         *behind),
        out_spaces=[HBM] * 5,
        scratch=[pltpu.VMEM((rows, width), BF16), pltpu.VMEM((1, width), F32),
                 pltpu.VMEM((1, width), F32), pltpu.SemaphoreType.DMA((5,))],
    )
    whole = lambda x: x.reshape(length, heads, width)
    return (
        whole(attended),
        whole(query_grad),
        whole(value_grad),
        threshold_grad[0],
        gain_grad[0],
    )


def solution(mesh):
    block = P("ctx", "head", None)
    return jax.shard_map(
        on_device,
        mesh=mesh,
        in_specs=(block, block, block, P(), P(), P("ctx"), block),
        out_specs=(block, block, block, P(), P()),
        check_vma=False,
    )
```

```python
import functools
import math

import jax
import jax.numpy as jnp
from jax import lax
from jax.experimental import pallas as pl
from jax.experimental.pallas import tpu as pltpu
from jax.sharding import PartitionSpec as P

BF16 = jnp.bfloat16
F32 = jnp.float32
MARK_ROWS = 8
VMEM_LIMIT = 48 * 1024 * 1024


def row_iota(shape):
    return lax.broadcasted_iota(jnp.int32, shape, 0)


def col_iota(shape):
    return lax.broadcasted_iota(jnp.int32, shape, 1)


def dot_nn(a, b):
    return lax.dot_general(a, b, (((1,), (0,)), ((), ())), preferred_element_type=F32)


def dot_nt(a, b):
    return lax.dot_general(a, b, (((1,), (1,)), ((), ())), preferred_element_type=F32)


def dot_tn(a, b):
    return lax.dot_general(a, b, (((0,), (0,)), ((), ())), preferred_element_type=F32)


def spread_heads(x, own_ref):
    return jnp.concatenate([x * own_ref[h] for h in range(own_ref.shape[0])], axis=1)


def put_message(out_ref, state, mark_ref):
    count, width = state.shape[0], out_ref.shape[1]
    for h in range(state.shape[1] // width):
        out_ref[h * count : (h + 1) * count, :] = state[:, h * width : (h + 1) * width]
    out_ref[out_ref.shape[0] - MARK_ROWS :, :] = mark_ref[...]


def take_messages(refs, mark_ref):
    total = None
    for ref in refs:
        count = ref.shape[0] - MARK_ROWS
        same = (ref[count : count + 1, :] == mark_ref[:1, :]).astype(F32)
        part = ref[:count, :] * same
        total = part if total is None else total + part
    return total.astype(BF16)


def side_by_side(state, heads):
    count = state.shape[0] // heads
    return jnp.concatenate([state[h * count : (h + 1) * count] for h in range(heads)], axis=1)


def pattern_kernel(heads, own_ref):
    head = lax.rem(row_iota(own_ref.shape[1:]), heads)
    for h in range(heads):
        own_ref[h] = (head == h).astype(BF16)


def marks_kernel(
    heads, ids_ref, threshold_ref, last_ref, tail_mark_ref, threshold_out_ref
):
    threshold_out_ref[...] = threshold_ref[...]
    ids = ids_ref[...]
    tail = ids[:, ids.shape[1] - 1 :]
    before_last = jnp.sum((ids != tail).astype(jnp.int32), axis=1, keepdims=True)
    last_ref[...] = (row_iota(last_ref.shape) >= heads * before_last).astype(F32)
    tail_mark_ref[...] = jnp.broadcast_to(tail.astype(F32), tail_mark_ref.shape)


def tail_kernel(
    heads, spikes_ref, values_ref, threshold_ref, last_ref, tail_mark_ref, own_ref, tail_ref, keys_ref
):
    keys = spikes_ref[...].astype(F32) * threshold_ref[...]
    keys_ref[...] = keys.astype(BF16)
    kept = (keys * last_ref[...]).astype(BF16)
    put_message(tail_ref, dot_tn(kept, spread_heads(values_ref[...], own_ref)), tail_mark_ref)


def inside_kernel(
    heads, queries_ref, keys_ref, values_ref, cotangent_ref, gain_ref, ids_ref, last_ref, own_ref,
    first_ref, head_mark_ref, base_ref, scores_t_ref, mask_ref, values_t_ref, first_queries_ref,
    first_queries_t_ref, last_keys_ref, upstream_ref, gain_out_ref,
):
    rows = queries_ref.shape[0]
    tokens = ids_ref.shape[1]
    queries = queries_ref[...]
    ids = ids_ref[...].astype(F32)
    head = ids[:, :1]
    in_first = jnp.sum((ids == head).astype(jnp.int32), axis=1, keepdims=True)
    first = (row_iota(first_ref.shape) < heads * in_first).astype(F32)
    first_ref[...] = first
    head_mark_ref[...] = jnp.broadcast_to(head, head_mark_ref.shape)
    apart = row_iota((rows, tokens)) - heads * col_iota((rows, tokens))
    down = jnp.sum(
        jnp.where((apart >= 0) & (apart < heads), ids, 0.0), axis=1, keepdims=True
    )
    r = row_iota((rows, rows))
    c = col_iota((rows, rows))
    across = jnp.sum(jnp.where(r == c, down, 0.0), axis=0, keepdims=True)
    together = (down == across) & (lax.rem(r - c, heads) == 0)
    allowed = (together & (c <= r)).astype(F32).astype(BF16)
    allowed_t = (together & (r <= c)).astype(F32).astype(BF16)
    keys = keys_ref[...]
    scores = dot_nt(queries, keys).astype(BF16) * allowed
    scores_t_ref[...] = dot_nt(keys, queries).astype(BF16) * allowed_t
    mask_ref[...] = allowed
    values_t_ref[...] = values_ref[...].T
    first_queries = spread_heads(
        (queries.astype(F32) * first).astype(BF16), own_ref
    )
    first_queries_ref[...] = first_queries
    first_queries_t_ref[...] = first_queries.T
    last_keys_ref[...] = spread_heads((keys.astype(F32) * last_ref[...]).astype(BF16), own_ref)
    gain_out_ref[...] = gain_ref[...]
    upstream_ref[...] = cotangent_ref[...].astype(F32) * gain_ref[...]
    base_ref[...] = queries.astype(F32) + dot_nn(scores, values_ref[...])


def middle_kernel(
    heads, hops, queries_ref, first_queries_ref, first_queries_t_ref, values_t_ref, cotangent_ref,
    upstream_ref, base_ref, mask_ref, keys_ref, threshold_ref, gain_ref, first_ref, head_mark_ref,
    own_ref, *refs,
):
    received = refs[:hops]
    attended_ref, query_grad_ref, gnorm_ref, back_ref, partial_ref = refs[hops:]
    rows, width = queries_ref.shape
    carried = take_messages(received, head_mark_ref)
    gain = gain_ref[...]
    first = first_ref[...]
    queries = queries_ref[...]
    mixed = base_ref[...] + dot_nn(first_queries_ref[...], carried)
    cotangent = cotangent_ref[...].astype(F32)
    upstream = upstream_ref[...]
    square = jnp.mean(mixed * mixed, axis=1, keepdims=True)
    inner = jnp.mean(mixed * upstream, axis=1, keepdims=True)
    ratio = lax.rsqrt(square + 1e-06)
    gnorm_f = ratio * upstream - mixed * (ratio * ratio * ratio * inner)
    gnorm = gnorm_f.astype(BF16)
    gnorm_ref[...] = gnorm
    spread = spread_heads((gnorm_f * first).astype(BF16), own_ref)
    half = rows // 2
    early = dot_nn(gnorm[:half], values_t_ref[:, :half]).astype(BF16) * mask_ref[:half, :half]
    late = dot_nn(gnorm[half:], values_t_ref[...]).astype(BF16) * mask_ref[half:, :]
    mixing = jnp.concatenate(
        [dot_nn(early, keys_ref[:half, :]), dot_nn(late, keys_ref[...])], axis=0
    ) + dot_nt(spread, side_by_side(carried, heads))
    query_grad_ref[...] = (gnorm.astype(F32) + mixing).astype(BF16)
    normed = mixed * ratio
    attended_ref[...] = (normed * gain).astype(BF16)
    gain_sum = jnp.sum(cotangent * normed, axis=0, keepdims=True)
    threshold_sum = jnp.sum(queries.astype(F32) * mixing, axis=0, keepdims=True)
    put_message(back_ref, dot_nn(first_queries_t_ref[...], gnorm), head_mark_ref)
    both = jnp.concatenate([threshold_sum / threshold_ref[...], gain_sum], axis=0)
    partial_ref[...] = jnp.broadcast_to(both[None], partial_ref.shape)


def last_kernel(
    heads, hops, scale, gnorm_ref, scores_t_ref, last_keys_ref, tail_mark_ref, parts_ref,
    attended_ref, query_grad_ref, *refs,
):
    received = refs[:hops]
    attended_hbm, query_grad_hbm, value_grad_hbm, threshold_hbm, gain_hbm = refs[hops : hops + 5]
    value_grad_ref, threshold_ref, gain_ref, sems = refs[hops + 5 :]
    copies = [
        pltpu.make_async_copy(attended_ref, attended_hbm, sems.at[0]),
        pltpu.make_async_copy(query_grad_ref, query_grad_hbm, sems.at[1]),
        pltpu.make_async_copy(value_grad_ref, value_grad_hbm, sems.at[2]),
        pltpu.make_async_copy(threshold_ref, threshold_hbm, sems.at[3]),
        pltpu.make_async_copy(gain_ref, gain_hbm, sems.at[4]),
    ]
    copies[0].start()
    copies[1].start()
    parts = parts_ref[...]
    even = lax.rem(row_iota(parts.shape), 2) == 0
    threshold_ref[...] = jnp.sum(jnp.where(even, parts, 0.0), axis=0, keepdims=True) * scale
    copies[3].start()
    gain_ref[...] = jnp.sum(jnp.where(even, 0.0, parts), axis=0, keepdims=True) * scale
    copies[4].start()
    returned = take_messages(received, tail_mark_ref)
    across = dot_nn(last_keys_ref[...], returned)
    value_grad_ref[...] = (dot_nn(scores_t_ref[...], gnorm_ref[...]) + across).astype(BF16)
    copies[2].start()
    for copy in copies:
        copy.wait()


VMEM = pl.BlockSpec(memory_space=pltpu.VMEM)
HBM = pl.BlockSpec(memory_space=pltpu.HBM)


def call(
    kernel, name, out, args, in_space=VMEM, out_spaces=None, scratch=(), flops=10**8, size=None
):
    if size is None:
        size = sum(a.size * a.dtype.itemsize for a in (*args, *out))
    return pl.pallas_call(
        kernel,
        name=name,
        out_shape=out,
        in_specs=[in_space] * len(args),
        out_specs=out_spaces or [VMEM] * len(out),
        scratch_shapes=list(scratch),
        compiler_params=pltpu.CompilerParams(vmem_limit_bytes=VMEM_LIMIT),
        cost_estimate=pl.CostEstimate(flops=flops, bytes_accessed=size, transcendentals=0),
    )(*args)


def shifted(x, by):
    count, lanes = lax.axis_size("ctx"), lax.axis_size("head")
    pairs = []
    for block in range(count):
        for lane in range(lanes):
            wraps = not 0 <= block + by < count
            swap = wraps and abs(by) == 2 and lanes % 2 == 0
            to = (block + by) % count * lanes + (lane ^ 1 if swap else lane)
            pairs.append((block * lanes + lane, to))
    return lax.ppermute(x, ("ctx", "head"), pairs)


def neighbours(message, reach, sign):
    if reach <= 3:
        order = range(reach, 0, -1) if sign > 0 else range(1, reach + 1)
        return [shifted(message, sign * by) for by in order]
    rows = message.shape[0] - MARK_ROWS
    state, marks = message[:rows], message[rows:]
    window = 1
    while window < reach:
        other = shifted(jnp.concatenate([state, marks]), sign * window)
        same = (other[rows:][:1] == marks[:1]).astype(F32)
        state = state + same * other[:rows]
        window = 2 * window
    return [shifted(jnp.concatenate([state, marks]), sign)]


def on_device(queries, spikes, values, threshold, norm_gain, document_ids, cotangent):
    length, heads, width = queries.shape
    rows = length * heads
    blocks = lax.axis_size("ctx")
    devices = blocks * lax.axis_size("head")
    reach = -(-(length * blocks // 4 - 1) // length)
    flat = lambda x: x.reshape(rows, width)
    q, s, v, ct = flat(queries), flat(spikes), flat(values), flat(cotangent)
    thr, gain, ids = threshold[None], norm_gain[None], document_ids[None]
    like = jax.ShapeDtypeStruct
    message = like((heads * width + MARK_ROWS, width), F32)
    flat_bf = like((rows, width), BF16)
    row_f = like((1, width), F32)

    flat_f = like((rows, width), F32)
    square = like((rows, rows), BF16)
    (own,) = call(
        functools.partial(pattern_kernel, heads),
        "pattern",
        [like((heads, rows, width), BF16)],
        (),
        flops=4 * 10**9,
    )
    mark = like((MARK_ROWS, width), F32)
    last, tail_mark, thr = call(
        functools.partial(marks_kernel, heads), "marks", [flat_f, mark, row_f], (ids, thr),
        flops=1, size=1,
    )
    tail, keys = call(
        functools.partial(tail_kernel, heads),
        "tail",
        [message, flat_bf],
        (s, v, thr, last, tail_mark, own),
    )
    ahead = neighbours(tail, reach, 1)
    wide = like((rows, heads * width), BF16)
    first, head_mark, base, scores_t, mask, v_t, first_q, first_q_t, last_k, upstream, gain = call(
        functools.partial(inside_kernel, heads),
        "inside",
        [flat_f, mark, flat_f, square, square, like((width, rows), BF16), wide, like((heads * width, rows), BF16),
         wide, flat_f, row_f],
        (q, keys, v, ct, gain, ids, last, own),
    )
    attended, query_grad, gnorm, back, partial = call(
        functools.partial(middle_kernel, heads, len(ahead)),
        "middle",
        [flat_bf, flat_bf, flat_bf, message, like((devices, 2, width), F32)],
        (q, first_q, first_q_t, v_t, ct, upstream, base, mask, keys, thr, gain, first, head_mark, own,
         *ahead),
    )
    behind = neighbours(back, reach, -1)
    parts = lax.all_to_all(partial, ("head", "ctx"), 0, 0)
    scale = 1.0 / math.sqrt(rows * devices)
    attended, query_grad, value_grad, threshold_grad, gain_grad = call(
        functools.partial(last_kernel, heads, len(behind), scale),
        "last",
        [flat_bf, flat_bf, flat_bf, row_f, row_f],
        (gnorm, scores_t, last_k, tail_mark, parts.reshape(2 * devices, width), attended, query_grad,
         *behind),
        out_spaces=[HBM] * 5,
        scratch=[pltpu.VMEM((rows, width), BF16), pltpu.VMEM((1, width), F32),
                 pltpu.VMEM((1, width), F32), pltpu.SemaphoreType.DMA((5,))],
    )
    whole = lambda x: x.reshape(length, heads, width)
    return (
        whole(attended),
        whole(query_grad),
        whole(value_grad),
        threshold_grad[0],
        gain_grad[0],
    )


def solution(mesh):
    block = P("ctx", "head", None)
    return jax.shard_map(
        on_device,
        mesh=mesh,
        in_specs=(block, block, block, P(), P(), P("ctx"), block),
        out_specs=(block, block, block, P(), P()),
        check_vma=False,
    )
```

```python
import functools
import math

import jax
import jax.numpy as jnp
from jax import lax
from jax.experimental import pallas as pl
from jax.experimental.pallas import tpu as pltpu
from jax.sharding import PartitionSpec as P

BF16 = jnp.bfloat16
F32 = jnp.float32
MARK_ROWS = 8
VMEM_LIMIT = 48 * 1024 * 1024


def row_iota(shape):
    return lax.broadcasted_iota(jnp.int32, shape, 0)


def col_iota(shape):
    return lax.broadcasted_iota(jnp.int32, shape, 1)


def dot_nn(a, b):
    return lax.dot_general(a, b, (((1,), (0,)), ((), ())), preferred_element_type=F32)


def dot_nt(a, b):
    return lax.dot_general(a, b, (((1,), (1,)), ((), ())), preferred_element_type=F32)


def dot_tn(a, b):
    return lax.dot_general(a, b, (((0,), (0,)), ((), ())), preferred_element_type=F32)


def spread_heads(x, own_ref):
    return jnp.concatenate([x * own_ref[h] for h in range(own_ref.shape[0])], axis=1)


def put_message(out_ref, state, mark_ref):
    count, width = state.shape[0], out_ref.shape[1]
    for h in range(state.shape[1] // width):
        out_ref[h * count : (h + 1) * count, :] = state[:, h * width : (h + 1) * width]
    out_ref[out_ref.shape[0] - MARK_ROWS :, :] = mark_ref[...]


def take_messages(refs, mark_ref):
    total = None
    for ref in refs:
        count = ref.shape[0] - MARK_ROWS
        same = (ref[count : count + 1, :] == mark_ref[:1, :]).astype(F32)
        part = ref[:count, :] * same
        total = part if total is None else total + part
    return total.astype(BF16)


def side_by_side(state, heads):
    count = state.shape[0] // heads
    return jnp.concatenate([state[h * count : (h + 1) * count] for h in range(heads)], axis=1)


def pattern_kernel(heads, own_ref):
    head = lax.rem(row_iota(own_ref.shape[1:]), heads)
    for h in range(heads):
        own_ref[h] = (head == h).astype(BF16)


def marks_kernel(
    heads, ids_ref, threshold_ref, last_ref, tail_mark_ref, threshold_out_ref
):
    threshold_out_ref[...] = threshold_ref[...]
    ids = ids_ref[...]
    tail = ids[:, ids.shape[1] - 1 :]
    before_last = jnp.sum((ids != tail).astype(jnp.int32), axis=1, keepdims=True)
    last_ref[...] = (row_iota(last_ref.shape) >= heads * before_last).astype(F32)
    tail_mark_ref[...] = jnp.broadcast_to(tail.astype(F32), tail_mark_ref.shape)


def tail_kernel(
    heads, spikes_ref, values_ref, threshold_ref, last_ref, tail_mark_ref, own_ref, tail_ref, keys_ref
):
    keys = spikes_ref[...].astype(F32) * threshold_ref[...]
    keys_ref[...] = keys.astype(BF16)
    kept = (keys * last_ref[...]).astype(BF16)
    put_message(tail_ref, dot_tn(kept, spread_heads(values_ref[...], own_ref)), tail_mark_ref)


def inside_kernel(
    heads, queries_ref, keys_ref, values_ref, cotangent_ref, gain_ref, ids_ref, last_ref, own_ref,
    head_mark_ref, base_ref, into_values_ref, mask_ref, values_t_ref, first_queries_ref,
    first_queries_t_ref, upstream_ref, own_first_ref, gain_out_ref,
):
    rows = queries_ref.shape[0]
    tokens = ids_ref.shape[1]
    queries = queries_ref[...]
    ids = ids_ref[...].astype(F32)
    head = ids[:, :1]
    in_first = jnp.sum((ids == head).astype(jnp.int32), axis=1, keepdims=True)
    first = (row_iota(base_ref.shape) < heads * in_first).astype(F32)
    head_mark_ref[...] = jnp.broadcast_to(head, head_mark_ref.shape)
    apart = row_iota((rows, tokens)) - heads * col_iota((rows, tokens))
    down = jnp.sum(
        jnp.where((apart >= 0) & (apart < heads), ids, 0.0), axis=1, keepdims=True
    )
    r = row_iota((rows, rows))
    c = col_iota((rows, rows))
    across = jnp.sum(jnp.where(r == c, down, 0.0), axis=0, keepdims=True)
    together = (down == across) & (lax.rem(r - c, heads) == 0)
    allowed = (together & (c <= r)).astype(F32).astype(BF16)
    allowed_t = (together & (r <= c)).astype(F32).astype(BF16)
    keys = keys_ref[...]
    scores = dot_nt(queries, keys).astype(BF16) * allowed
    wide = dot_nt(keys, queries).astype(BF16) * allowed_t
    mask_ref[...] = allowed
    values_t_ref[...] = values_ref[...].T
    first_queries = spread_heads(
        (queries.astype(F32) * first).astype(BF16), own_ref
    )
    first_queries_ref[...] = first_queries
    first_queries_t_ref[...] = first_queries.T
    into_values_ref[:, :rows] = wide
    into_values_ref[:, rows:] = spread_heads(
        (keys.astype(F32) * last_ref[...]).astype(BF16), own_ref
    )
    for h in range(heads):
        own_first_ref[h] = (own_ref[h].astype(F32) * first).astype(BF16)
    gain_out_ref[...] = gain_ref[...]
    upstream_ref[...] = cotangent_ref[...].astype(F32) * gain_ref[...]
    base_ref[...] = queries.astype(F32) + dot_nn(scores, values_ref[...])


def middle_kernel(
    heads, hops, queries_ref, first_queries_ref, first_queries_t_ref, values_t_ref, cotangent_ref,
    upstream_ref, base_ref, mask_ref, keys_ref, threshold_ref, gain_ref, head_mark_ref,
    own_first_ref, *refs,
):
    received = refs[:hops]
    attended_ref, query_grad_ref, gnorm_ref, back_ref, partial_ref = refs[hops:]
    rows, width = queries_ref.shape
    carried = take_messages(received, head_mark_ref)
    gain = gain_ref[...]
    queries = queries_ref[...]
    mixed = base_ref[...] + dot_nn(first_queries_ref[...], carried)
    cotangent = cotangent_ref[...].astype(F32)
    upstream = upstream_ref[...]
    square = jnp.mean(mixed * mixed, axis=1, keepdims=True)
    inner = jnp.mean(mixed * upstream, axis=1, keepdims=True)
    ratio = lax.rsqrt(square + 1e-06)
    gnorm = (ratio * upstream - mixed * (ratio * ratio * ratio * inner)).astype(BF16)
    gnorm_ref[...] = gnorm
    spread = spread_heads(gnorm, own_first_ref)
    half = rows // 2
    early = dot_nn(gnorm[:half], values_t_ref[:, :half]).astype(BF16) * mask_ref[:half, :half]
    late = dot_nn(gnorm[half:], values_t_ref[...]).astype(BF16) * mask_ref[half:, :]
    back_states = side_by_side(carried, heads).T
    mixing = jnp.concatenate(
        [
            dot_nn(
                jnp.concatenate([early, spread[:half]], axis=1),
                jnp.concatenate([keys_ref[:half, :], back_states], axis=0),
            ),
            dot_nn(
                jnp.concatenate([late, spread[half:]], axis=1),
                jnp.concatenate([keys_ref[...], back_states], axis=0),
            ),
        ],
        axis=0,
    )
    query_grad_ref[...] = (gnorm.astype(F32) + mixing).astype(BF16)
    normed = mixed * ratio
    attended_ref[...] = (normed * gain).astype(BF16)
    gain_sum = jnp.sum(cotangent * normed, axis=0, keepdims=True)
    threshold_sum = jnp.sum(queries.astype(F32) * mixing, axis=0, keepdims=True)
    put_message(back_ref, dot_nn(first_queries_t_ref[...], gnorm), head_mark_ref)
    both = jnp.concatenate([threshold_sum / threshold_ref[...], gain_sum], axis=0)
    partial_ref[...] = jnp.broadcast_to(both[None], partial_ref.shape)


def last_kernel(
    heads, hops, scale, gnorm_ref, into_values_ref, tail_mark_ref, parts_ref,
    attended_ref, query_grad_ref, *refs,
):
    received = refs[:hops]
    attended_hbm, query_grad_hbm, value_grad_hbm, threshold_hbm, gain_hbm = refs[hops : hops + 5]
    value_grad_ref, threshold_ref, gain_ref, sems = refs[hops + 5 :]
    copies = [
        pltpu.make_async_copy(attended_ref, attended_hbm, sems.at[0]),
        pltpu.make_async_copy(query_grad_ref, query_grad_hbm, sems.at[1]),
        pltpu.make_async_copy(value_grad_ref, value_grad_hbm, sems.at[2]),
        pltpu.make_async_copy(threshold_ref, threshold_hbm, sems.at[3]),
        pltpu.make_async_copy(gain_ref, gain_hbm, sems.at[4]),
    ]
    copies[0].start()
    copies[1].start()
    parts = parts_ref[...]
    even = lax.rem(row_iota(parts.shape), 2) == 0
    threshold_ref[...] = jnp.sum(jnp.where(even, parts, 0.0), axis=0, keepdims=True) * scale
    copies[3].start()
    gain_ref[...] = jnp.sum(jnp.where(even, 0.0, parts), axis=0, keepdims=True) * scale
    copies[4].start()
    returned = take_messages(received, tail_mark_ref)
    sources = jnp.concatenate([gnorm_ref[...], returned], axis=0)
    value_grad_ref[...] = dot_nn(into_values_ref[...], sources).astype(BF16)
    copies[2].start()
    for copy in copies:
        copy.wait()


VMEM = pl.BlockSpec(memory_space=pltpu.VMEM)
HBM = pl.BlockSpec(memory_space=pltpu.HBM)


def call(
    kernel, name, out, args, in_space=VMEM, out_spaces=None, scratch=(), flops=10**8, size=None
):
    if size is None:
        size = sum(a.size * a.dtype.itemsize for a in (*args, *out))
    return pl.pallas_call(
        kernel,
        name=name,
        out_shape=out,
        in_specs=[in_space] * len(args),
        out_specs=out_spaces or [VMEM] * len(out),
        scratch_shapes=list(scratch),
        compiler_params=pltpu.CompilerParams(vmem_limit_bytes=VMEM_LIMIT),
        cost_estimate=pl.CostEstimate(flops=flops, bytes_accessed=size, transcendentals=0),
    )(*args)


def shifted(x, by):
    count, lanes = lax.axis_size("ctx"), lax.axis_size("head")
    pairs = []
    for block in range(count):
        for lane in range(lanes):
            wraps = not 0 <= block + by < count
            swap = wraps and abs(by) == 2 and lanes % 2 == 0
            to = (block + by) % count * lanes + (lane ^ 1 if swap else lane)
            pairs.append((block * lanes + lane, to))
    return lax.ppermute(x, ("ctx", "head"), pairs)


def neighbours(message, reach, sign):
    if reach <= 3:
        order = range(reach, 0, -1) if sign > 0 else range(1, reach + 1)
        return [shifted(message, sign * by) for by in order]
    rows = message.shape[0] - MARK_ROWS
    state, marks = message[:rows], message[rows:]
    window = 1
    while window < reach:
        other = shifted(jnp.concatenate([state, marks]), sign * window)
        same = (other[rows:][:1] == marks[:1]).astype(F32)
        state = state + same * other[:rows]
        window = 2 * window
    return [shifted(jnp.concatenate([state, marks]), sign)]


def on_device(queries, spikes, values, threshold, norm_gain, document_ids, cotangent):
    length, heads, width = queries.shape
    rows = length * heads
    blocks = lax.axis_size("ctx")
    devices = blocks * lax.axis_size("head")
    reach = -(-(length * blocks // 4 - 1) // length)
    flat = lambda x: x.reshape(rows, width)
    q, s, v, ct = flat(queries), flat(spikes), flat(values), flat(cotangent)
    thr, gain, ids = threshold[None], norm_gain[None], document_ids[None]
    like = jax.ShapeDtypeStruct
    message = like((heads * width + MARK_ROWS, width), F32)
    flat_bf = like((rows, width), BF16)
    row_f = like((1, width), F32)

    flat_f = like((rows, width), F32)
    square = like((rows, rows), BF16)
    (own,) = call(
        functools.partial(pattern_kernel, heads),
        "pattern",
        [like((heads, rows, width), BF16)],
        (),
        flops=4 * 10**9,
    )
    mark = like((MARK_ROWS, width), F32)
    last, tail_mark, thr = call(
        functools.partial(marks_kernel, heads), "marks", [flat_f, mark, row_f], (ids, thr),
        flops=1, size=1,
    )
    tail, keys = call(
        functools.partial(tail_kernel, heads),
        "tail",
        [message, flat_bf],
        (s, v, thr, last, tail_mark, own),
    )
    ahead = neighbours(tail, reach, 1)
    wide = like((rows, heads * width), BF16)
    head_mark, base, into_v, mask, v_t, first_q, first_q_t, upstream, own_first, gain = call(
        functools.partial(inside_kernel, heads),
        "inside",
        [mark, flat_f, like((rows, rows + heads * width), BF16), square, like((width, rows), BF16),
         wide, like((heads * width, rows), BF16), flat_f, like((heads, rows, width), BF16), row_f],
        (q, keys, v, ct, gain, ids, last, own),
    )
    attended, query_grad, gnorm, back, partial = call(
        functools.partial(middle_kernel, heads, len(ahead)),
        "middle",
        [flat_bf, flat_bf, flat_bf, message, like((devices, 2, width), F32)],
        (q, first_q, first_q_t, v_t, ct, upstream, base, mask, keys, thr, gain, head_mark, own_first,
         *ahead),
    )
    behind = neighbours(back, reach, -1)
    parts = lax.all_to_all(partial, ("head", "ctx"), 0, 0)
    scale = 1.0 / math.sqrt(rows * devices)
    attended, query_grad, value_grad, threshold_grad, gain_grad = call(
        functools.partial(last_kernel, heads, len(behind), scale),
        "last",
        [flat_bf, flat_bf, flat_bf, row_f, row_f],
        (gnorm, into_v, tail_mark, parts.reshape(2 * devices, width), attended, query_grad,
         *behind),
        out_spaces=[HBM] * 5,
        scratch=[pltpu.VMEM((rows, width), BF16), pltpu.VMEM((1, width), F32),
                 pltpu.VMEM((1, width), F32), pltpu.SemaphoreType.DMA((5,))],
    )
    whole = lambda x: x.reshape(length, heads, width)
    return (
        whole(attended),
        whole(query_grad),
        whole(value_grad),
        threshold_grad[0],
        gain_grad[0],
    )


def solution(mesh):
    block = P("ctx", "head", None)
    return jax.shard_map(
        on_device,
        mesh=mesh,
        in_specs=(block, block, block, P(), P(), P("ctx"), block),
        out_specs=(block, block, block, P(), P()),
        check_vma=False,
    )
```

```python
import functools
import math

import jax
import jax.numpy as jnp
from jax import lax
from jax.experimental import pallas as pl
from jax.experimental.pallas import tpu as pltpu
from jax.sharding import PartitionSpec as P

BF16 = jnp.bfloat16
F32 = jnp.float32
MARK_ROWS = 8
VMEM_LIMIT = 48 * 1024 * 1024


def row_iota(shape):
    return lax.broadcasted_iota(jnp.int32, shape, 0)


def col_iota(shape):
    return lax.broadcasted_iota(jnp.int32, shape, 1)


def dot_nn(a, b):
    return lax.dot_general(a, b, (((1,), (0,)), ((), ())), preferred_element_type=F32)


def dot_nt(a, b):
    return lax.dot_general(a, b, (((1,), (1,)), ((), ())), preferred_element_type=F32)


def dot_tn(a, b):
    return lax.dot_general(a, b, (((0,), (0,)), ((), ())), preferred_element_type=F32)


def spread_heads(x, own_ref):
    return jnp.concatenate([x * own_ref[h] for h in range(own_ref.shape[0])], axis=1)


def put_message(out_ref, state, mark_ref):
    count, width = state.shape[0], out_ref.shape[1]
    for h in range(state.shape[1] // width):
        out_ref[h * count : (h + 1) * count, :] = state[:, h * width : (h + 1) * width]
    out_ref[out_ref.shape[0] - MARK_ROWS :, :] = mark_ref[...]


def take_messages(refs, mark_ref):
    total = None
    for ref in refs:
        count = ref.shape[0] - MARK_ROWS
        same = (ref[count : count + 1, :] == mark_ref[:1, :]).astype(F32)
        part = ref[:count, :] * same
        total = part if total is None else total + part
    return total.astype(BF16)


def side_by_side(state, heads):
    count = state.shape[0] // heads
    return jnp.concatenate([state[h * count : (h + 1) * count] for h in range(heads)], axis=1)


def opening_kernel(zero_ref):
    zero_ref[...] = jnp.zeros_like(zero_ref)


def marks_kernel(
    heads, ids_ref, threshold_ref, zero_ref, last_ref, tail_mark_ref, threshold_out_ref, own_ref
):
    threshold_out_ref[...] = threshold_ref[...]
    head = lax.rem(row_iota(own_ref.shape[1:]), heads)
    for h in range(heads):
        own_ref[h] = (head == h).astype(BF16)
    ids = ids_ref[...]
    tail = ids[:, ids.shape[1] - 1 :]
    before_last = jnp.sum((ids != tail).astype(jnp.int32), axis=1, keepdims=True)
    last_ref[...] = (row_iota(last_ref.shape) >= heads * before_last).astype(F32)
    tail_mark_ref[...] = jnp.broadcast_to(tail.astype(F32), tail_mark_ref.shape)


def tail_kernel(
    heads, spikes_ref, values_ref, threshold_ref, last_ref, tail_mark_ref, own_ref, tail_ref, keys_ref
):
    keys = spikes_ref[...].astype(F32) * threshold_ref[...]
    keys_ref[...] = keys.astype(BF16)
    kept = (keys * last_ref[...]).astype(BF16)
    put_message(tail_ref, dot_tn(kept, spread_heads(values_ref[...], own_ref)), tail_mark_ref)


def inside_kernel(
    heads, queries_ref, keys_ref, values_ref, cotangent_ref, gain_ref, ids_ref, last_ref, own_ref,
    head_mark_ref, base_ref, into_values_ref, mask_ref, values_t_ref, first_queries_ref,
    first_queries_t_ref, upstream_ref, own_first_ref, gain_out_ref,
):
    rows = queries_ref.shape[0]
    tokens = ids_ref.shape[1]
    queries = queries_ref[...]
    ids = ids_ref[...].astype(F32)
    head = ids[:, :1]
    in_first = jnp.sum((ids == head).astype(jnp.int32), axis=1, keepdims=True)
    first = (row_iota(base_ref.shape) < heads * in_first).astype(F32)
    head_mark_ref[...] = jnp.broadcast_to(head, head_mark_ref.shape)
    apart = row_iota((rows, tokens)) - heads * col_iota((rows, tokens))
    down = jnp.sum(
        jnp.where((apart >= 0) & (apart < heads), ids, 0.0), axis=1, keepdims=True
    )
    r = row_iota((rows, rows))
    c = col_iota((rows, rows))
    across = jnp.sum(jnp.where(r == c, down, 0.0), axis=0, keepdims=True)
    together = (down == across) & (lax.rem(r - c, heads) == 0)
    allowed = (together & (c <= r)).astype(F32).astype(BF16)
    allowed_t = (together & (r <= c)).astype(F32).astype(BF16)
    keys = keys_ref[...]
    scores = dot_nt(queries, keys).astype(BF16) * allowed
    wide = dot_nt(keys, queries).astype(BF16) * allowed_t
    mask_ref[...] = allowed
    values_t_ref[...] = values_ref[...].T
    first_queries = spread_heads(
        (queries.astype(F32) * first).astype(BF16), own_ref
    )
    first_queries_ref[...] = first_queries
    first_queries_t_ref[...] = first_queries.T
    into_values_ref[:, :rows] = wide
    into_values_ref[:, rows:] = spread_heads(
        (keys.astype(F32) * last_ref[...]).astype(BF16), own_ref
    )
    for h in range(heads):
        own_first_ref[h] = (own_ref[h].astype(F32) * first).astype(BF16)
    gain_out_ref[...] = gain_ref[...]
    upstream_ref[...] = cotangent_ref[...].astype(F32) * gain_ref[...]
    base_ref[...] = queries.astype(F32) + dot_nn(scores, values_ref[...])


def middle_kernel(
    heads, hops, queries_ref, first_queries_ref, first_queries_t_ref, values_t_ref, cotangent_ref,
    upstream_ref, base_ref, mask_ref, keys_ref, threshold_ref, gain_ref, head_mark_ref,
    own_first_ref, *refs,
):
    received = refs[:hops]
    attended_ref, query_grad_ref, gnorm_ref, back_ref, partial_ref = refs[hops:]
    rows, width = queries_ref.shape
    carried = take_messages(received, head_mark_ref)
    gain = gain_ref[...]
    queries = queries_ref[...]
    mixed = base_ref[...] + dot_nn(first_queries_ref[...], carried)
    cotangent = cotangent_ref[...].astype(F32)
    upstream = upstream_ref[...]
    square = jnp.mean(mixed * mixed, axis=1, keepdims=True)
    inner = jnp.mean(mixed * upstream, axis=1, keepdims=True)
    ratio = lax.rsqrt(square + 1e-06)
    gnorm = (ratio * upstream - mixed * (ratio * ratio * ratio * inner)).astype(BF16)
    gnorm_ref[...] = gnorm
    spread = spread_heads(gnorm, own_first_ref)
    half = rows // 2
    early = dot_nn(gnorm[:half], values_t_ref[:, :half]).astype(BF16) * mask_ref[:half, :half]
    late = dot_nn(gnorm[half:], values_t_ref[...]).astype(BF16) * mask_ref[half:, :]
    back_states = side_by_side(carried, heads).T
    mixing = jnp.concatenate(
        [
            dot_nn(
                jnp.concatenate([early, spread[:half]], axis=1),
                jnp.concatenate([keys_ref[:half, :], back_states], axis=0),
            ),
            dot_nn(
                jnp.concatenate([late, spread[half:]], axis=1),
                jnp.concatenate([keys_ref[...], back_states], axis=0),
            ),
        ],
        axis=0,
    )
    query_grad_ref[...] = (gnorm.astype(F32) + mixing).astype(BF16)
    normed = mixed * ratio
    attended_ref[...] = (normed * gain).astype(BF16)
    gain_sum = jnp.sum(cotangent * normed, axis=0, keepdims=True)
    threshold_sum = jnp.sum(queries.astype(F32) * mixing, axis=0, keepdims=True)
    put_message(back_ref, dot_nn(first_queries_t_ref[...], gnorm), head_mark_ref)
    both = jnp.concatenate([threshold_sum / threshold_ref[...], gain_sum], axis=0)
    partial_ref[...] = jnp.broadcast_to(both[None], partial_ref.shape)


def last_kernel(
    heads, hops, scale, gnorm_ref, into_values_ref, tail_mark_ref, parts_ref,
    attended_ref, query_grad_ref, *refs,
):
    received = refs[:hops]
    attended_hbm, query_grad_hbm, value_grad_hbm, threshold_hbm, gain_hbm = refs[hops : hops + 5]
    value_grad_ref, threshold_ref, gain_ref, sems = refs[hops + 5 :]
    copies = [
        pltpu.make_async_copy(attended_ref, attended_hbm, sems.at[0]),
        pltpu.make_async_copy(query_grad_ref, query_grad_hbm, sems.at[1]),
        pltpu.make_async_copy(value_grad_ref, value_grad_hbm, sems.at[2]),
        pltpu.make_async_copy(threshold_ref, threshold_hbm, sems.at[3]),
        pltpu.make_async_copy(gain_ref, gain_hbm, sems.at[4]),
    ]
    copies[0].start()
    copies[1].start()
    parts = parts_ref[...]
    even = lax.rem(row_iota(parts.shape), 2) == 0
    threshold_ref[...] = jnp.sum(jnp.where(even, parts, 0.0), axis=0, keepdims=True) * scale
    copies[3].start()
    gain_ref[...] = jnp.sum(jnp.where(even, 0.0, parts), axis=0, keepdims=True) * scale
    copies[4].start()
    returned = take_messages(received, tail_mark_ref)
    sources = jnp.concatenate([gnorm_ref[...], returned], axis=0)
    value_grad_ref[...] = dot_nn(into_values_ref[...], sources).astype(BF16)
    copies[2].start()
    for copy in copies:
        copy.wait()


VMEM = pl.BlockSpec(memory_space=pltpu.VMEM)
HBM = pl.BlockSpec(memory_space=pltpu.HBM)


def call(
    kernel, name, out, args, in_space=VMEM, out_spaces=None, scratch=(), flops=10**8, size=None
):
    if size is None:
        size = sum(a.size * a.dtype.itemsize for a in (*args, *out))
    return pl.pallas_call(
        kernel,
        name=name,
        out_shape=out,
        in_specs=[in_space] * len(args),
        out_specs=out_spaces or [VMEM] * len(out),
        scratch_shapes=list(scratch),
        compiler_params=pltpu.CompilerParams(vmem_limit_bytes=VMEM_LIMIT),
        cost_estimate=pl.CostEstimate(flops=flops, bytes_accessed=size, transcendentals=0),
    )(*args)


def shifted(x, by):
    count, lanes = lax.axis_size("ctx"), lax.axis_size("head")
    pairs = []
    for block in range(count):
        for lane in range(lanes):
            wraps = not 0 <= block + by < count
            swap = wraps and abs(by) == 2 and lanes % 2 == 0
            to = (block + by) % count * lanes + (lane ^ 1 if swap else lane)
            pairs.append((block * lanes + lane, to))
    return lax.ppermute(x, ("ctx", "head"), pairs)


def neighbours(message, reach, sign):
    if reach <= 3:
        order = range(reach, 0, -1) if sign > 0 else range(1, reach + 1)
        return [shifted(message, sign * by) for by in order]
    rows = message.shape[0] - MARK_ROWS
    state, marks = message[:rows], message[rows:]
    window = 1
    while window < reach:
        other = shifted(jnp.concatenate([state, marks]), sign * window)
        same = (other[rows:][:1] == marks[:1]).astype(F32)
        state = state + same * other[:rows]
        window = 2 * window
    return [shifted(jnp.concatenate([state, marks]), sign)]


def on_device(queries, spikes, values, threshold, norm_gain, document_ids, cotangent):
    length, heads, width = queries.shape
    rows = length * heads
    blocks = lax.axis_size("ctx")
    devices = blocks * lax.axis_size("head")
    reach = -(-(length * blocks // 4 - 1) // length)
    flat = lambda x: x.reshape(rows, width)
    q, s, v, ct = flat(queries), flat(spikes), flat(values), flat(cotangent)
    thr, gain, ids = threshold[None], norm_gain[None], document_ids[None]
    like = jax.ShapeDtypeStruct
    message = like((heads * width + MARK_ROWS, width), F32)
    flat_bf = like((rows, width), BF16)
    row_f = like((1, width), F32)

    flat_f = like((rows, width), F32)
    square = like((rows, rows), BF16)
    (zero,) = call(
        opening_kernel, "opening", [like((8, 128), F32)], (), flops=4 * 10**9
    )
    mark = like((MARK_ROWS, width), F32)
    last, tail_mark, thr, own = call(
        functools.partial(marks_kernel, heads), "marks", [flat_f, mark, row_f, like((heads, rows, width), BF16)], (ids, thr, zero),
        flops=1, size=1,
    )
    tail, keys = call(
        functools.partial(tail_kernel, heads),
        "tail",
        [message, flat_bf],
        (s, v, thr, last, tail_mark, own),
    )
    ahead = neighbours(tail, reach, 1)
    wide = like((rows, heads * width), BF16)
    head_mark, base, into_v, mask, v_t, first_q, first_q_t, upstream, own_first, gain = call(
        functools.partial(inside_kernel, heads),
        "inside",
        [mark, flat_f, like((rows, rows + heads * width), BF16), square, like((width, rows), BF16),
         wide, like((heads * width, rows), BF16), flat_f, like((heads, rows, width), BF16), row_f],
        (q, keys, v, ct, gain, ids, last, own),
    )
    attended, query_grad, gnorm, back, partial = call(
        functools.partial(middle_kernel, heads, len(ahead)),
        "middle",
        [flat_bf, flat_bf, flat_bf, message, like((devices, 2, width), F32)],
        (q, first_q, first_q_t, v_t, ct, upstream, base, mask, keys, thr, gain, head_mark, own_first,
         *ahead),
    )
    behind = neighbours(back, reach, -1)
    parts = lax.all_to_all(partial, ("head", "ctx"), 0, 0)
    scale = 1.0 / math.sqrt(rows * devices)
    attended, query_grad, value_grad, threshold_grad, gain_grad = call(
        functools.partial(last_kernel, heads, len(behind), scale),
        "last",
        [flat_bf, flat_bf, flat_bf, row_f, row_f],
        (gnorm, into_v, tail_mark, parts.reshape(2 * devices, width), attended, query_grad,
         *behind),
        out_spaces=[HBM] * 5,
        scratch=[pltpu.VMEM((rows, width), BF16), pltpu.VMEM((1, width), F32),
                 pltpu.VMEM((1, width), F32), pltpu.SemaphoreType.DMA((5,))],
    )
    whole = lambda x: x.reshape(length, heads, width)
    return (
        whole(attended),
        whole(query_grad),
        whole(value_grad),
        threshold_grad[0],
        gain_grad[0],
    )


def solution(mesh):
    block = P("ctx", "head", None)
    return jax.shard_map(
        on_device,
        mesh=mesh,
        in_specs=(block, block, block, P(), P(), P("ctx"), block),
        out_specs=(block, block, block, P(), P()),
        check_vma=False,
    )
```

```python
import functools
import math

import jax
import jax.numpy as jnp
from jax import lax
from jax.experimental import pallas as pl
from jax.experimental.pallas import tpu as pltpu
from jax.sharding import PartitionSpec as P

BF16 = jnp.bfloat16
F32 = jnp.float32
MARK_ROWS = 8
VMEM_LIMIT = 48 * 1024 * 1024


def row_iota(shape):
    return lax.broadcasted_iota(jnp.int32, shape, 0)


def col_iota(shape):
    return lax.broadcasted_iota(jnp.int32, shape, 1)


def dot_nn(a, b):
    return lax.dot_general(a, b, (((1,), (0,)), ((), ())), preferred_element_type=F32)


def dot_nt(a, b):
    return lax.dot_general(a, b, (((1,), (1,)), ((), ())), preferred_element_type=F32)


def dot_tn(a, b):
    return lax.dot_general(a, b, (((0,), (0,)), ((), ())), preferred_element_type=F32)


def spread_heads(x, own_ref):
    return jnp.concatenate([x * own_ref[h] for h in range(own_ref.shape[0])], axis=1)


def put_message(out_ref, state, mark_ref):
    count, width = state.shape[0], out_ref.shape[1]
    for h in range(state.shape[1] // width):
        out_ref[h * count : (h + 1) * count, :] = state[:, h * width : (h + 1) * width]
    out_ref[out_ref.shape[0] - MARK_ROWS :, :] = mark_ref[...]


def take_messages(refs, mark_ref):
    total = None
    for ref in refs:
        count = ref.shape[0] - MARK_ROWS
        same = (ref[count : count + 1, :] == mark_ref[:1, :]).astype(F32)
        part = ref[:count, :] * same
        total = part if total is None else total + part
    return total.astype(BF16)


def side_by_side(state, heads):
    count = state.shape[0] // heads
    return jnp.concatenate([state[h * count : (h + 1) * count] for h in range(heads)], axis=1)


def pattern_kernel(heads, own_ref):
    head = lax.rem(row_iota(own_ref.shape[1:]), heads)
    for h in range(heads):
        own_ref[h] = (head == h).astype(BF16)


def marks_kernel(
    heads, ids_ref, threshold_ref, last_ref, tail_mark_ref, threshold_out_ref
):
    threshold_out_ref[...] = threshold_ref[...]
    ids = ids_ref[...]
    tail = ids[:, ids.shape[1] - 1 :]
    before_last = jnp.sum((ids != tail).astype(jnp.int32), axis=1, keepdims=True)
    last_ref[...] = (row_iota(last_ref.shape) >= heads * before_last).astype(F32)
    tail_mark_ref[...] = jnp.broadcast_to(tail.astype(F32), tail_mark_ref.shape)


def tail_kernel(
    heads, spikes_ref, values_ref, threshold_ref, last_ref, tail_mark_ref, own_ref, tail_ref, keys_ref
):
    keys = spikes_ref[...].astype(F32) * threshold_ref[...]
    keys_ref[...] = keys.astype(BF16)
    kept = (keys * last_ref[...]).astype(BF16)
    put_message(tail_ref, dot_tn(kept, spread_heads(values_ref[...], own_ref)), tail_mark_ref)


def inside_kernel(
    heads, queries_ref, keys_ref, values_ref, cotangent_ref, gain_ref, ids_ref, last_ref, own_ref,
    first_ref, head_mark_ref, base_ref, scores_t_ref, mask_ref, values_t_ref, first_queries_ref,
    first_queries_t_ref, last_keys_ref, upstream_ref, gain_out_ref,
):
    rows = queries_ref.shape[0]
    tokens = ids_ref.shape[1]
    queries = queries_ref[...]
    ids = ids_ref[...].astype(F32)
    head = ids[:, :1]
    in_first = jnp.sum((ids == head).astype(jnp.int32), axis=1, keepdims=True)
    first = (row_iota(first_ref.shape) < heads * in_first).astype(F32)
    first_ref[...] = first
    head_mark_ref[...] = jnp.broadcast_to(head, head_mark_ref.shape)
    apart = row_iota((rows, tokens)) - heads * col_iota((rows, tokens))
    down = jnp.sum(
        jnp.where((apart >= 0) & (apart < heads), ids, 0.0), axis=1, keepdims=True
    )
    r = row_iota((rows, rows))
    c = col_iota((rows, rows))
    across = jnp.sum(jnp.where(r == c, down, 0.0), axis=0, keepdims=True)
    together = (down == across) & (lax.rem(r - c, heads) == 0)
    allowed = (together & (c <= r)).astype(F32).astype(BF16)
    allowed_t = (together & (r <= c)).astype(F32).astype(BF16)
    keys = keys_ref[...]
    scores = dot_nt(queries, keys).astype(BF16) * allowed
    scores_t_ref[...] = dot_nt(keys, queries).astype(BF16) * allowed_t
    mask_ref[...] = allowed
    values_t_ref[...] = values_ref[...].T
    first_queries = spread_heads(
        (queries.astype(F32) * first).astype(BF16), own_ref
    )
    first_queries_ref[...] = first_queries
    first_queries_t_ref[...] = first_queries.T
    last_keys_ref[...] = spread_heads((keys.astype(F32) * last_ref[...]).astype(BF16), own_ref)
    gain_out_ref[...] = gain_ref[...]
    upstream_ref[...] = cotangent_ref[...].astype(F32) * gain_ref[...]
    base_ref[...] = queries.astype(F32) + dot_nn(scores, values_ref[...])


def middle_kernel(
    heads, hops, queries_ref, first_queries_ref, first_queries_t_ref, values_t_ref, cotangent_ref,
    upstream_ref, base_ref, mask_ref, keys_ref, threshold_ref, gain_ref, first_ref, head_mark_ref,
    own_ref, *refs,
):
    received = refs[:hops]
    attended_ref, query_grad_ref, gnorm_ref, back_ref, partial_ref = refs[hops:]
    rows, width = queries_ref.shape
    carried = take_messages(received, head_mark_ref)
    gain = gain_ref[...]
    first = first_ref[...]
    queries = queries_ref[...]
    mixed = base_ref[...] + dot_nn(first_queries_ref[...], carried)
    cotangent = cotangent_ref[...].astype(F32)
    upstream = upstream_ref[...]
    square = jnp.mean(mixed * mixed, axis=1, keepdims=True)
    inner = jnp.mean(mixed * upstream, axis=1, keepdims=True)
    ratio = lax.rsqrt(square + 1e-06)
    gnorm_f = ratio * upstream - mixed * (ratio * ratio * ratio * inner)
    gnorm = gnorm_f.astype(BF16)
    gnorm_ref[...] = gnorm
    spread = spread_heads((gnorm_f * first).astype(BF16), own_ref)
    half = rows // 2
    early = dot_nn(gnorm[:half], values_t_ref[:, :half]).astype(BF16) * mask_ref[:half, :half]
    late = dot_nn(gnorm[half:], values_t_ref[...]).astype(BF16) * mask_ref[half:, :]
    mixing = jnp.concatenate(
        [dot_nn(early, keys_ref[:half, :]), dot_nn(late, keys_ref[...])], axis=0
    ) + dot_nt(spread, side_by_side(carried, heads))
    query_grad_ref[...] = (gnorm.astype(F32) + mixing).astype(BF16)
    normed = mixed * ratio
    attended_ref[...] = (normed * gain).astype(BF16)
    gain_sum = jnp.sum(cotangent * normed, axis=0, keepdims=True)
    threshold_sum = jnp.sum(queries.astype(F32) * mixing, axis=0, keepdims=True)
    put_message(back_ref, dot_nn(first_queries_t_ref[...], gnorm), head_mark_ref)
    both = jnp.concatenate([threshold_sum / threshold_ref[...], gain_sum], axis=0)
    partial_ref[...] = jnp.broadcast_to(both[None], partial_ref.shape)


def last_kernel(
    heads, hops, scale, gnorm_ref, scores_t_ref, last_keys_ref, tail_mark_ref, parts_ref,
    attended_ref, query_grad_ref, *refs,
):
    received = refs[:hops]
    attended_hbm, query_grad_hbm, value_grad_hbm, threshold_hbm, gain_hbm = refs[hops : hops + 5]
    value_grad_ref, threshold_ref, gain_ref, sems = refs[hops + 5 :]
    copies = [
        pltpu.make_async_copy(attended_ref, attended_hbm, sems.at[0]),
        pltpu.make_async_copy(query_grad_ref, query_grad_hbm, sems.at[1]),
        pltpu.make_async_copy(value_grad_ref, value_grad_hbm, sems.at[2]),
        pltpu.make_async_copy(threshold_ref, threshold_hbm, sems.at[3]),
        pltpu.make_async_copy(gain_ref, gain_hbm, sems.at[4]),
    ]
    copies[0].start()
    copies[1].start()
    parts = parts_ref[...]
    even = lax.rem(row_iota(parts.shape), 2) == 0
    threshold_ref[...] = jnp.sum(jnp.where(even, parts, 0.0), axis=0, keepdims=True) * scale
    copies[3].start()
    gain_ref[...] = jnp.sum(jnp.where(even, 0.0, parts), axis=0, keepdims=True) * scale
    copies[4].start()
    returned = take_messages(received, tail_mark_ref)
    across = dot_nn(last_keys_ref[...], returned)
    value_grad_ref[...] = (dot_nn(scores_t_ref[...], gnorm_ref[...]) + across).astype(BF16)
    copies[2].start()
    for copy in copies:
        copy.wait()


VMEM = pl.BlockSpec(memory_space=pltpu.VMEM)
HBM = pl.BlockSpec(memory_space=pltpu.HBM)


def call(
    kernel, name, out, args, in_space=VMEM, out_spaces=None, scratch=(), flops=10**8, size=None
):
    if size is None:
        size = sum(a.size * a.dtype.itemsize for a in (*args, *out))
    return pl.pallas_call(
        kernel,
        name=name,
        out_shape=out,
        in_specs=[in_space] * len(args),
        out_specs=out_spaces or [VMEM] * len(out),
        scratch_shapes=list(scratch),
        compiler_params=pltpu.CompilerParams(vmem_limit_bytes=VMEM_LIMIT),
        cost_estimate=pl.CostEstimate(flops=flops, bytes_accessed=size, transcendentals=0),
    )(*args)


def shifted(x, by):
    count, lanes = lax.axis_size("ctx"), lax.axis_size("head")
    pairs = []
    for block in range(count):
        for lane in range(lanes):
            wraps = not 0 <= block + by < count
            swap = wraps and abs(by) == 2 and lanes % 2 == 0
            target = (block + by) % count
            if swap and by == 2 and count % 2 == 0:
                target = target ^ 1
            to = target * lanes + (lane ^ 1 if swap else lane)
            pairs.append((block * lanes + lane, to))
    return lax.ppermute(x, ("ctx", "head"), pairs)


def neighbours(message, reach, sign):
    if reach <= 3:
        order = range(reach, 0, -1) if sign > 0 else range(1, reach + 1)
        return [shifted(message, sign * by) for by in order]
    rows = message.shape[0] - MARK_ROWS
    state, marks = message[:rows], message[rows:]
    window = 1
    while window < reach:
        other = shifted(jnp.concatenate([state, marks]), sign * window)
        same = (other[rows:][:1] == marks[:1]).astype(F32)
        state = state + same * other[:rows]
        window = 2 * window
    return [shifted(jnp.concatenate([state, marks]), sign)]


def on_device(queries, spikes, values, threshold, norm_gain, document_ids, cotangent):
    length, heads, width = queries.shape
    rows = length * heads
    blocks = lax.axis_size("ctx")
    devices = blocks * lax.axis_size("head")
    reach = -(-(length * blocks // 4 - 1) // length)
    flat = lambda x: x.reshape(rows, width)
    q, s, v, ct = flat(queries), flat(spikes), flat(values), flat(cotangent)
    thr, gain, ids = threshold[None], norm_gain[None], document_ids[None]
    like = jax.ShapeDtypeStruct
    message = like((heads * width + MARK_ROWS, width), F32)
    flat_bf = like((rows, width), BF16)
    row_f = like((1, width), F32)

    flat_f = like((rows, width), F32)
    square = like((rows, rows), BF16)
    (own,) = call(
        functools.partial(pattern_kernel, heads),
        "pattern",
        [like((heads, rows, width), BF16)],
        (),
        flops=4 * 10**9,
    )
    mark = like((MARK_ROWS, width), F32)
    last, tail_mark, thr = call(
        functools.partial(marks_kernel, heads), "marks", [flat_f, mark, row_f], (ids, thr),
        flops=1, size=1,
    )
    tail, keys = call(
        functools.partial(tail_kernel, heads),
        "tail",
        [message, flat_bf],
        (s, v, thr, last, tail_mark, own),
    )
    ahead = neighbours(tail, reach, 1)
    wide = like((rows, heads * width), BF16)
    first, head_mark, base, scores_t, mask, v_t, first_q, first_q_t, last_k, upstream, gain = call(
        functools.partial(inside_kernel, heads),
        "inside",
        [flat_f, mark, flat_f, square, square, like((width, rows), BF16), wide, like((heads * width, rows), BF16),
         wide, flat_f, row_f],
        (q, keys, v, ct, gain, ids, last, own),
    )
    attended, query_grad, gnorm, back, partial = call(
        functools.partial(middle_kernel, heads, len(ahead)),
        "middle",
        [flat_bf, flat_bf, flat_bf, message, like((devices, 2, width), F32)],
        (q, first_q, first_q_t, v_t, ct, upstream, base, mask, keys, thr, gain, first, head_mark, own,
         *ahead),
    )
    behind = neighbours(back, reach, -1)
    parts = lax.all_to_all(partial, ("head", "ctx"), 0, 0)
    scale = 1.0 / math.sqrt(rows * devices)
    attended, query_grad, value_grad, threshold_grad, gain_grad = call(
        functools.partial(last_kernel, heads, len(behind), scale),
        "last",
        [flat_bf, flat_bf, flat_bf, row_f, row_f],
        (gnorm, scores_t, last_k, tail_mark, parts.reshape(2 * devices, width), attended, query_grad,
         *behind),
        out_spaces=[HBM] * 5,
        scratch=[pltpu.VMEM((rows, width), BF16), pltpu.VMEM((1, width), F32),
                 pltpu.VMEM((1, width), F32), pltpu.SemaphoreType.DMA((5,))],
    )
    whole = lambda x: x.reshape(length, heads, width)
    return (
        whole(attended),
        whole(query_grad),
        whole(value_grad),
        threshold_grad[0],
        gain_grad[0],
    )


def solution(mesh):
    block = P("ctx", "head", None)
    return jax.shard_map(
        on_device,
        mesh=mesh,
        in_specs=(block, block, block, P(), P(), P("ctx"), block),
        out_specs=(block, block, block, P(), P()),
        check_vma=False,
    )
```
